128 devices in a mesh: ctx: 16 (over x, z), tp: 8 (over y, core).
Axes of the slice: x: 4, y: 4, z: 4, core: 2. Of those that a mesh axis runs over, the one named last changes fastest.
Arguments:
- queries: bfloat16 [8192, 8192], P('ctx', 'tp'), may hold values from -5 to 5
- keys: bfloat16 [8192, 1024], P('ctx', 'tp'), may hold values from -5 to 5
- values: bfloat16 [8192, 1024], P('ctx', 'tp'), may hold values from -6 to 6
- outputs: bfloat16 [8192, 8192], P('ctx', 'tp'), may hold values from -2 to 2
- out_grad: bfloat16 [8192, 8192], P('ctx', 'tp'), may hold values from -6 to 6
- lengths: int32 [8], replicated, may hold values from 1 to 4608, 8192 in all
- w_query: bfloat16 [5120, 8192], P(None, 'tp'), may hold values from -0.078125 to 0.078125
- w_key: bfloat16 [5120, 1024], P(None, 'tp'), may hold values from -0.078125 to 0.078125
- w_value: bfloat16 [5120, 1024], P(None, 'tp'), may hold values from -0.078125 to 0.078125
Outputs:
- input_grad: bfloat16 [8192, 5120], P('ctx', 'tp')
The draws below stay inside these ranges and needn't reach their ends.
All inputs are finite; a program needn't handle non-finite values.
Results may differ from the reference program's by a relative error of at most 0.02.
Values may be sent and summed in bfloat16 or wider, within the bound.
A program may use at most 128 MiB of HBM per device.

```python
import math
import jax
import jax.numpy as jnp
import numpy as np
from jax import lax

D = 5120
HEADS = 64
KV_HEADS = 8
HD = 128
TOKENS = 8192
NDOCS = 8
LONGEST = 4608


def paired_fields(key):
    key_qn = jax.random.fold_in(key, 0)
    key_kn = jax.random.fold_in(key, 2)
    key_pick = jax.random.fold_in(key, 4)
    query_field = jnp.clip(jax.random.normal(key_qn, (TOKENS, HEADS * HD)), -4.0, 4.0)
    key_field = jnp.clip(jax.random.normal(key_kn, (TOKENS, KV_HEADS * HD)), -4.0, 4.0)
    spacing = TOKENS // 3
    picked_rows = jnp.arange(3, dtype=jnp.int32) * spacing + jax.random.randint(key_pick, (3,), 1, spacing)
    key_field = key_field.at[picked_rows].set(key_field[picked_rows])
    key_field = key_field.at[picked_rows - 1].set(key_field[picked_rows - 1])
    query_field = query_field.at[picked_rows].set(query_field[picked_rows])
    return (query_field, key_field)


def draw_queries(key, part):
    fields = paired_fields(key)
    return fields[0].astype(jnp.bfloat16)


def draw_keys(key, part):
    fields = paired_fields(key)
    return fields[1].astype(jnp.bfloat16)


def block_levels(key, extent, pieces, low, high):
    factor_of, own = 1.0, jax.random.fold_in(key, 6)
    for axis_at, blocks in pieces:
        steps = jnp.exp(jax.random.uniform(jax.random.fold_in(own, axis_at), (blocks,), jnp.float32, low / len(pieces), high / len(pieces)))
        factor_of = factor_of * jnp.repeat(steps, extent[axis_at] // blocks).reshape([-1 if axis == axis_at else 1 for axis in range(len(extent))])
    return factor_of


def profile(amount, total, reach, slope):
    portions = [(1 << 20) // math.isqrt(grade ** slope) + 1 for grade in range(2, amount + 1)]
    spare, given = total - reach - (amount - 1), [1] * (amount - 1)
    while spare > 0:
        free = [i for i in range(amount - 1) if given[i] < reach]
        mass, budget = sum([portions[i] for i in free]), spare
        for i in free:
            extra = min(reach - given[i], max(1, budget * portions[i] // mass), spare)
            given[i] = given[i] + extra
            spare = spare - extra
    return np.array([reach] + given)


def ragged_sizes(rng, number_of, total, limit, slope):
    if number_of == 2:
        one = jax.random.randint(rng, (), max(1, total - limit), min(limit, total - 1) + 1)
        return jnp.stack([one, total - one])
    tallies = jnp.asarray(profile(number_of, total, limit, slope), jnp.int32)
    pairs = (number_of - 1) // 2
    source_of, taker = tallies[1:1 + 2 * pairs:2], tallies[2:2 + 2 * pairs:2]
    room = jnp.minimum(source_of - 1, limit - taker)
    shifted = jax.random.randint(jax.random.fold_in(rng, 1), (pairs,), 0, 1 << 20) % (room + 1)
    tallies = tallies.at[1:1 + 2 * pairs:2].set(source_of - shifted).at[2:2 + 2 * pairs:2].set(taker + shifted)
    return tallies[jax.random.permutation(jax.random.fold_in(rng, 2), number_of)]


def noise(rng, dims, scale, limit, pieces=(), kind=jnp.bfloat16):
    values = scale * jax.random.normal(rng, dims, jnp.float32)
    if pieces:
        values = values * block_levels(rng, dims, pieces, -0.22, 0.18)
    return jnp.clip(values, -limit, limit).astype(kind)


def setup_inputs(seed: int = 0) -> dict:
    splits = jax.random.split(jax.random.key(seed), 10)
    return {
        "queries": draw_queries(jax.random.fold_in(splits[9], 71), 0),
        "keys": draw_keys(jax.random.fold_in(splits[9], 71), 0),
        "values": noise(splits[2], (TOKENS, KV_HEADS * HD), 1.0, 6.0, ((0, 16), (1, 8))),
        "outputs": noise(splits[3], (TOKENS, HEADS * HD), 0.3, 2.0, ((0, 16), (1, 8))),
        "out_grad": noise(splits[4], (TOKENS, HEADS * HD), 1.0, 6.0, ((0, 16), (1, 8))),
        "lengths": ragged_sizes(splits[5], NDOCS, TOKENS, LONGEST, 2).astype(jnp.int32),
        "w_query": noise(splits[6], (D, HEADS * HD), D ** -0.5, 0.078125, ((1, 8),)),
        "w_key": noise(splits[7], (D, KV_HEADS * HD), D ** -0.5, 0.078125, ((1, 8),)),
        "w_value": noise(splits[8], (D, KV_HEADS * HD), D ** -0.5, 0.078125, ((1, 8),)),
    }


def reference(queries, keys, values, outputs, out_grad, lengths, w_query, w_key, w_value):
    group_size = HEADS // KV_HEADS
    score_scale = HD ** -0.5
    doc_ends = jnp.cumsum(lengths, dtype=jnp.int32)
    positions = jnp.arange(TOKENS, dtype=jnp.int32)
    doc_of = jnp.sum((positions[:, None] >= doc_ends[None, :]).astype(jnp.int32), axis=1, dtype=jnp.int32)
    allowed = (positions[None, :] <= positions[:, None]) & (doc_of[None, :] == doc_of[:, None])
    query_heads = queries.astype(jnp.float32).reshape(TOKENS, HEADS, HD).transpose(1, 0, 2)
    output_heads = outputs.astype(jnp.float32).reshape(TOKENS, HEADS, HD).transpose(1, 0, 2)
    grad_heads = out_grad.astype(jnp.float32).reshape(TOKENS, HEADS, HD).transpose(1, 0, 2)
    key_heads = keys.astype(jnp.float32).reshape(TOKENS, KV_HEADS, HD).transpose(1, 0, 2)
    value_heads = values.astype(jnp.float32).reshape(TOKENS, KV_HEADS, HD).transpose(1, 0, 2)

    def one_head(head_index):
        shared = head_index // group_size
        query_head = query_heads[head_index]
        grad_head = grad_heads[head_index]
        output_head = output_heads[head_index]
        key_head = key_heads[shared]
        value_head = value_heads[shared]
        scores = jnp.dot(query_head, key_head.T) * score_scale
        scores = jnp.where(allowed, scores, -1e30)
        row_top = jnp.max(scores, axis=1, keepdims=True)
        exp_weights = jnp.where(allowed, jnp.exp(scores - row_top), 0.0)
        probability = exp_weights / jnp.sum(exp_weights, axis=1, keepdims=True)
        prob_low = lax.optimization_barrier(probability.astype(jnp.bfloat16)).astype(jnp.float32)
        prob_grad = jnp.dot(grad_head, value_head.T)
        row_delta = jnp.sum(grad_head * output_head, axis=1, keepdims=True)
        score_grad = probability * (prob_grad - row_delta)
        score_low = lax.optimization_barrier(score_grad.astype(jnp.bfloat16)).astype(jnp.float32)
        query_grad = score_scale * jnp.dot(score_low, key_head)
        key_grad = score_scale * jnp.dot(score_low.T, query_head)
        value_grad = jnp.dot(prob_low.T, grad_head)
        return query_grad, key_grad, value_grad

    query_grads, key_grads, value_grads = lax.map(one_head, jnp.arange(HEADS, dtype=jnp.int32))
    query_grad = query_grads.transpose(1, 0, 2).reshape(TOKENS, HEADS * HD).astype(jnp.bfloat16)
    key_grad = key_grads.reshape(KV_HEADS, group_size, TOKENS, HD).sum(axis=1)
    key_grad = key_grad.transpose(1, 0, 2).reshape(TOKENS, KV_HEADS * HD).astype(jnp.bfloat16)
    value_grad = value_grads.reshape(KV_HEADS, group_size, TOKENS, HD).sum(axis=1)
    value_grad = value_grad.transpose(1, 0, 2).reshape(TOKENS, KV_HEADS * HD).astype(jnp.bfloat16)
    summed = jnp.dot(query_grad, w_query.T, preferred_element_type=jnp.float32)
    summed = summed + jnp.dot(key_grad, w_key.T, preferred_element_type=jnp.float32)
    summed = summed + jnp.dot(value_grad, w_value.T, preferred_element_type=jnp.float32)
    return summed.astype(jnp.bfloat16)
```

```python
import functools
import jax, jax.numpy as jnp
from jax import lax
from jax.experimental import pallas as pl
from jax.experimental.pallas import tpu as pltpu
from jax.sharding import PartitionSpec as P

HD = 128
CHUNK = 128
TILE = 256
NEG = -1e30
SAFE = 60.0
LAST = (((1,), (1,)), ((), ()))


def attention_kernel(total, start_ref, lengths_ref, q_ref, do_ref, delta_ref, k_ref, v_ref,
                     dq_ref, dk_ref, dv_ref, e_ref, ds_ref, mt_ref, q_rows, do_rows, q_over, do_over, kt_ref, dqt_ref,
                     dk_acc, dv_acc, stat_ref):
    rows = q_rows.shape[0]
    heads = rows // CHUNK
    pair = 2 * CHUNK
    pairs = rows // pair
    chunks = q_ref.shape[0] // CHUNK
    tiles = total // TILE
    scale = HD ** -0.5
    to_log2 = scale * 1.4426950408889634

    dk_acc[...] = jnp.zeros_like(dk_acc)
    dv_acc[...] = jnp.zeros_like(dv_acc)

    def turn_keys(i, most):
        turned = k_ref[pl.ds(pl.multiple_of(i * TILE, TILE), TILE), :].T
        kt_ref[i] = turned
        wide = turned.astype(jnp.float32)
        return jnp.maximum(most, jnp.sum(wide * wide, axis=0, keepdims=True))

    key_most = jnp.max(lax.fori_loop(0, tiles, turn_keys, jnp.zeros((1, TILE), jnp.float32)))

    def one_chunk(j, _):
        first = start_ref[j]
        t0 = pl.multiple_of(j * CHUNK, CHUNK)
        query_most = jnp.zeros((CHUNK, 1), jnp.float32)
        for h in range(heads):
            part = q_ref[pl.ds(t0, CHUNK), h * HD:(h + 1) * HD]
            q_rows[h * CHUNK:(h + 1) * CHUNK, :] = part
            do_rows[h * CHUNK:(h + 1) * CHUNK, :] = do_ref[pl.ds(t0, CHUNK), h * HD:(h + 1) * HD]
            wide = part.astype(jnp.float32)
            query_most = jnp.maximum(query_most, jnp.sum(wide * wide, axis=1, keepdims=True))
        small = jnp.max(query_most) * key_most * (to_log2 * to_log2) <= SAFE * SAFE
        query_pos = first + lax.broadcasted_iota(jnp.int32, (1, pair), 1) % CHUNK
        row_start = jnp.zeros((1, pair), jnp.int32)
        low, high = jnp.int32(0), jnp.int32(0)
        begin = jnp.int32(0)
        for d in range(lengths_ref.shape[0]):
            row_start = jnp.where(query_pos >= begin, begin, row_start)
            low = jnp.where(first >= begin, begin, low)
            high = jnp.where(first + CHUNK - 1 >= begin, begin, high)
            begin = begin + lengths_ref[d]
        tile_low = low // TILE
        tile_end = (first + CHUNK - 1) // TILE + 1
        plain_low = jnp.minimum((high + TILE - 1) // TILE, tile_end)
        plain_end = jnp.maximum((first + 1) // TILE, plain_low)
        edge = plain_low - tile_low
        edges = edge + tile_end - plain_end

        def edge_tile(n):
            return jnp.where(n < edge, tile_low + n, plain_end + n - edge)

        def allowed_of(key0):
            key_pos = key0 + lax.broadcasted_iota(jnp.int32, (TILE, pair), 0)
            return (key_pos >= row_start) & (key_pos <= query_pos)

        def scores(key, p):
            return lax.dot_general(key, q_rows[p * pair:(p + 1) * pair, :], LAST,
                                   preferred_element_type=jnp.float32) * to_log2

        def weigh(i, sums, masked):
            key0 = pl.multiple_of(i * TILE, TILE)
            key = k_ref[pl.ds(key0, TILE), :]
            new = []
            for p in range(pairs):
                e = jnp.exp2(scores(key, p))
                if masked:
                    e = jnp.where(allowed_of(key0), e, 0.0)
                new.append(sums[p] + jnp.sum(e.reshape(TILE // 8, 8, pair), axis=0))
                e_ref[i - tile_low, :, p * pair:(p + 1) * pair] = e.astype(jnp.bfloat16)
            return tuple(new)

        @pl.when(small)
        def _():
            sums = tuple(jnp.zeros((8, pair), jnp.float32) for _ in range(pairs))
            sums = lax.fori_loop(0, edges, lambda n, s: weigh(edge_tile(n), s, True), sums)
            sums = lax.fori_loop(plain_low, plain_end, lambda i, s: weigh(i, s, False), sums)
            for p in range(pairs):
                stat_ref[:, p * pair:(p + 1) * pair] = 1.0 / jnp.sum(sums[p], axis=0, keepdims=True)

        @pl.when(jnp.logical_not(small))
        def _():
            def step(i, carry):
                tops, sums = carry
                key0 = pl.multiple_of(i * TILE, TILE)
                key = k_ref[pl.ds(key0, TILE), :]
                new_tops, new_sums = [], []
                for p in range(pairs):
                    s = jnp.where(allowed_of(key0), scores(key, p), NEG)
                    top = jnp.maximum(tops[p], jnp.max(s, axis=0, keepdims=True))
                    e = jnp.exp2(s - top)
                    new_sums.append(sums[p] * jnp.exp2(tops[p] - top) + jnp.sum(e, axis=0, keepdims=True))
                    new_tops.append(top)
                    e_ref[i - tile_low, :, p * pair:(p + 1) * pair] = e.astype(jnp.bfloat16)
                    mt_ref[i - tile_low, :, p * pair:(p + 1) * pair] = top
                return tuple(new_tops), tuple(new_sums)

            tops, sums = lax.fori_loop(tile_low, tile_end, step, (
                tuple(jnp.full((1, pair), NEG, jnp.float32) for _ in range(pairs)),
                tuple(jnp.zeros((1, pair), jnp.float32) for _ in range(pairs))))

            def settle(i, _):
                for p in range(pairs):
                    part = slice(p * pair, (p + 1) * pair)
                    factor = jnp.exp2(mt_ref[i - tile_low, :, part] - tops[p])
                    e_ref[i - tile_low, :, part] = (
                        e_ref[i - tile_low, :, part].astype(jnp.float32) * factor).astype(jnp.bfloat16)
                return 0

            lax.fori_loop(tile_low, tile_end, settle, 0)
            for p in range(pairs):
                stat_ref[:, p * pair:(p + 1) * pair] = 1.0 / sums[p]

        for h in range(heads):
            part = slice(h * CHUNK, (h + 1) * CHUNK)
            inverse = jnp.broadcast_to(stat_ref[:, part], (HD, CHUNK)).T
            q_over[part, :] = (q_rows[part, :].astype(jnp.float32) * inverse).astype(jnp.bfloat16)
            do_over[part, :] = (do_rows[part, :].astype(jnp.float32) * inverse).astype(jnp.bfloat16)
        delta = [jnp.concatenate([delta_ref[2 * p:2 * p + 1, pl.ds(t0, CHUNK)],
                                  delta_ref[2 * p + 1:2 * p + 2, pl.ds(t0, CHUNK)]], axis=1) for p in range(pairs)]
        dqt_ref[...] = jnp.zeros_like(dqt_ref)

        def grad_step(i, _):
            key0 = pl.multiple_of(i * TILE, TILE)
            slot = i - tile_low
            value = v_ref[pl.ds(key0, TILE), :]
            key_t = kt_ref[i]
            for p in range(pairs):
                part = slice(p * pair, (p + 1) * pair)
                dp = lax.dot_general(value, do_rows[part, :], LAST, preferred_element_type=jnp.float32)
                ds_ref[:, part] = (e_ref[slot, :, part].astype(jnp.float32) * (dp - delta[p])).astype(jnp.bfloat16)
            dv_acc[pl.ds(key0, TILE), :] += jnp.dot(e_ref[slot], do_over[...], preferred_element_type=jnp.float32)
            dk_acc[pl.ds(key0, TILE), :] += jnp.dot(ds_ref[...], q_over[...], preferred_element_type=jnp.float32)
            dqt_ref[...] += jnp.dot(key_t, ds_ref[...], preferred_element_type=jnp.float32)
            return 0

        lax.fori_loop(tile_low, tile_end, grad_step, 0)
        for h in range(heads):
            part = slice(h * CHUNK, (h + 1) * CHUNK)
            dq_ref[pl.ds(t0, CHUNK), h * HD:(h + 1) * HD] = (
                dqt_ref[:, part] * (stat_ref[:, part] * scale)).T.astype(jnp.bfloat16)
        return 0

    lax.fori_loop(0, chunks, one_chunk, 0)

    def write(i, _):
        at = pl.ds(pl.multiple_of(i * TILE, TILE), TILE)
        dk_ref[at, :] = (dk_acc[at, :] * scale).astype(jnp.bfloat16)
        dv_ref[at, :] = dv_acc[at, :].astype(jnp.bfloat16)
        return 0

    lax.fori_loop(0, tiles, write, 0)


def attention(starts, lengths, q, do, delta, k, v, longest=4608):
    total = k.shape[0]
    rows = q.shape[1] // HD * CHUNK
    max_tiles = (longest + CHUNK) // TILE + 2
    vmem = pl.BlockSpec(memory_space=pltpu.VMEM)
    smem = pl.BlockSpec(memory_space=pltpu.SMEM)
    return pl.pallas_call(
        functools.partial(attention_kernel, total),
        out_shape=[jax.ShapeDtypeStruct(q.shape, jnp.bfloat16),
                   jax.ShapeDtypeStruct(k.shape, jnp.bfloat16),
                   jax.ShapeDtypeStruct(k.shape, jnp.bfloat16)],
        in_specs=[smem, smem] + [vmem] * 5,
        out_specs=[vmem] * 3,
        scratch_shapes=[
            pltpu.VMEM((max_tiles, TILE, rows), jnp.bfloat16),
            pltpu.VMEM((TILE, rows), jnp.bfloat16),
            pltpu.VMEM((max_tiles, 1, rows), jnp.float32),
            pltpu.VMEM((rows, HD), jnp.bfloat16),
            pltpu.VMEM((rows, HD), jnp.bfloat16),
            pltpu.VMEM((rows, HD), jnp.bfloat16),
            pltpu.VMEM((rows, HD), jnp.bfloat16),
            pltpu.VMEM((total // TILE, HD, TILE), jnp.bfloat16),
            pltpu.VMEM((HD, rows), jnp.float32),
            pltpu.VMEM((total, HD), jnp.float32),
            pltpu.VMEM((total, HD), jnp.float32),
            pltpu.VMEM((1, rows), jnp.float32),
        ],
        compiler_params=pltpu.CompilerParams(vmem_limit_bytes=60 * 2**20),
        name="attention",
    )(starts, lengths, q, do, delta, k, v)


def shards(queries, keys, values, outputs, out_grad, lengths, w_query, w_key, w_value):
    row_count = queries.shape[0]
    heads = queries.shape[1] // HD
    me = lax.axis_index("ctx")
    starts = me * row_count + jnp.arange(row_count // CHUNK, dtype=jnp.int32) * CHUNK
    delta = jnp.sum(
        (out_grad.astype(jnp.float32) * outputs.astype(jnp.float32)).reshape(row_count, heads, HD), axis=2
    ).T
    collected = lax.all_gather(jnp.stack([keys, values]), "ctx", axis=1, tiled=True)
    query_grad, key_terms, value_terms = attention(
        starts, lengths, queries, out_grad, delta, collected[0], collected[1]
    )
    devices = lax.axis_size("ctx")
    partials = jnp.stack(
        [key_terms.reshape(devices, row_count, HD), value_terms.reshape(devices, row_count, HD)], axis=1
    )
    summed = lax.psum_scatter(partials, "ctx", scatter_dimension=0, tiled=True)[0]
    contract = (((1,), (1,)), ((), ()))
    total = lax.dot_general(query_grad, w_query, contract, preferred_element_type=jnp.float32)
    total = total + lax.dot_general(summed[0], w_key, contract, preferred_element_type=jnp.float32)
    total = total + lax.dot_general(summed[1], w_value, contract, preferred_element_type=jnp.float32)
    return lax.psum_scatter(total.astype(jnp.bfloat16), "tp", scatter_dimension=1, tiled=True)


def solution(mesh):
    in_specs = (P("ctx", "tp"),) * 5 + (P(),) + (P(None, "tp"),) * 3
    return jax.shard_map(shards, mesh=mesh, in_specs=in_specs, out_specs=P("ctx", "tp"), check_vma=False)
```

```python
import functools
import jax, jax.numpy as jnp
from jax import lax
from jax.experimental import pallas as pl
from jax.experimental.pallas import tpu as pltpu
from jax.sharding import PartitionSpec as P

HD = 128
CHUNK = 128
TILE = 256
NEG = -1e30
SAFE = 60.0
LAST = (((1,), (1,)), ((), ()))


def attention_kernel(total, start_ref, lengths_ref, q_ref, do_ref, delta_ref, kv_ref,
                     dq_ref, dkv_ref, e_ref, ds_ref, mt_ref, q_rows, do_rows, q_over, do_over, kt_ref, dqt_ref,
                     dk_acc, dv_acc, stat_ref):
    rows = q_rows.shape[0]
    heads = rows // CHUNK
    pair = 2 * CHUNK
    pairs = rows // pair
    chunks = q_ref.shape[0] // CHUNK
    tiles = total // TILE
    scale = HD ** -0.5
    to_log2 = scale * 1.4426950408889634

    dk_acc[...] = jnp.zeros_like(dk_acc)
    dv_acc[...] = jnp.zeros_like(dv_acc)

    def turn_keys(i, most):
        turned = kv_ref[pl.ds(pl.multiple_of(i * TILE, TILE), TILE), :HD].T
        kt_ref[i] = turned
        wide = turned.astype(jnp.float32)
        return jnp.maximum(most, jnp.sum(wide * wide, axis=0, keepdims=True))

    key_most = jnp.max(lax.fori_loop(0, tiles, turn_keys, jnp.zeros((1, TILE), jnp.float32)))

    def one_chunk(j, _):
        first = start_ref[j]
        t0 = pl.multiple_of(j * CHUNK, CHUNK)
        query_most = jnp.zeros((CHUNK, 1), jnp.float32)
        for h in range(heads):
            part = q_ref[pl.ds(t0, CHUNK), h * HD:(h + 1) * HD]
            q_rows[h * CHUNK:(h + 1) * CHUNK, :] = part
            do_rows[h * CHUNK:(h + 1) * CHUNK, :] = do_ref[pl.ds(t0, CHUNK), h * HD:(h + 1) * HD]
            wide = part.astype(jnp.float32)
            query_most = jnp.maximum(query_most, jnp.sum(wide * wide, axis=1, keepdims=True))
        small = jnp.max(query_most) * key_most * (to_log2 * to_log2) <= SAFE * SAFE
        query_pos = first + lax.broadcasted_iota(jnp.int32, (1, pair), 1) % CHUNK
        row_start = jnp.zeros((1, pair), jnp.int32)
        low, high = jnp.int32(0), jnp.int32(0)
        begin = jnp.int32(0)
        for d in range(lengths_ref.shape[0]):
            row_start = jnp.where(query_pos >= begin, begin, row_start)
            low = jnp.where(first >= begin, begin, low)
            high = jnp.where(first + CHUNK - 1 >= begin, begin, high)
            begin = begin + lengths_ref[d]
        tile_low = low // TILE
        tile_end = (first + CHUNK - 1) // TILE + 1
        plain_low = jnp.minimum((high + TILE - 1) // TILE, tile_end)
        plain_end = jnp.maximum((first + 1) // TILE, plain_low)
        edge = plain_low - tile_low
        edges = edge + tile_end - plain_end

        def edge_tile(n):
            return jnp.where(n < edge, tile_low + n, plain_end + n - edge)

        def allowed_of(key0):
            key_pos = key0 + lax.broadcasted_iota(jnp.int32, (TILE, pair), 0)
            return (key_pos >= row_start) & (key_pos <= query_pos)

        def scores(key, p):
            return lax.dot_general(key, q_rows[p * pair:(p + 1) * pair, :], LAST,
                                   preferred_element_type=jnp.float32) * to_log2

        def weigh(i, sums, masked):
            key0 = pl.multiple_of(i * TILE, TILE)
            key = kv_ref[pl.ds(key0, TILE), :HD]
            new = []
            for p in range(pairs):
                e = jnp.exp2(scores(key, p))
                if masked:
                    e = jnp.where(allowed_of(key0), e, 0.0)
                new.append(sums[p] + jnp.sum(e.reshape(TILE // 8, 8, pair), axis=0))
                e_ref[i - tile_low, :, p * pair:(p + 1) * pair] = e.astype(jnp.bfloat16)
            return tuple(new)

        @pl.when(small)
        def _():
            sums = tuple(jnp.zeros((8, pair), jnp.float32) for _ in range(pairs))
            sums = lax.fori_loop(0, edges, lambda n, s: weigh(edge_tile(n), s, True), sums)
            sums = lax.fori_loop(plain_low, plain_end, lambda i, s: weigh(i, s, False), sums)
            for p in range(pairs):
                stat_ref[:, p * pair:(p + 1) * pair] = 1.0 / jnp.sum(sums[p], axis=0, keepdims=True)

        @pl.when(jnp.logical_not(small))
        def _():
            def step(i, carry):
                tops, sums = carry
                key0 = pl.multiple_of(i * TILE, TILE)
                key = kv_ref[pl.ds(key0, TILE), :HD]
                new_tops, new_sums = [], []
                for p in range(pairs):
                    s = jnp.where(allowed_of(key0), scores(key, p), NEG)
                    top = jnp.maximum(tops[p], jnp.max(s, axis=0, keepdims=True))
                    e = jnp.exp2(s - top)
                    new_sums.append(sums[p] * jnp.exp2(tops[p] - top) + jnp.sum(e, axis=0, keepdims=True))
                    new_tops.append(top)
                    e_ref[i - tile_low, :, p * pair:(p + 1) * pair] = e.astype(jnp.bfloat16)
                    mt_ref[i - tile_low, :, p * pair:(p + 1) * pair] = top
                return tuple(new_tops), tuple(new_sums)

            tops, sums = lax.fori_loop(tile_low, tile_end, step, (
                tuple(jnp.full((1, pair), NEG, jnp.float32) for _ in range(pairs)),
                tuple(jnp.zeros((1, pair), jnp.float32) for _ in range(pairs))))

            def settle(i, _):
                for p in range(pairs):
                    part = slice(p * pair, (p + 1) * pair)
                    factor = jnp.exp2(mt_ref[i - tile_low, :, part] - tops[p])
                    e_ref[i - tile_low, :, part] = (
                        e_ref[i - tile_low, :, part].astype(jnp.float32) * factor).astype(jnp.bfloat16)
                return 0

            lax.fori_loop(tile_low, tile_end, settle, 0)
            for p in range(pairs):
                stat_ref[:, p * pair:(p + 1) * pair] = 1.0 / sums[p]

        for h in range(heads):
            part = slice(h * CHUNK, (h + 1) * CHUNK)
            inverse = jnp.broadcast_to(stat_ref[:, part], (HD, CHUNK)).T
            q_over[part, :] = (q_rows[part, :].astype(jnp.float32) * inverse).astype(jnp.bfloat16)
            do_over[part, :] = (do_rows[part, :].astype(jnp.float32) * inverse).astype(jnp.bfloat16)
        delta = [jnp.concatenate([delta_ref[2 * p:2 * p + 1, pl.ds(t0, CHUNK)],
                                  delta_ref[2 * p + 1:2 * p + 2, pl.ds(t0, CHUNK)]], axis=1) for p in range(pairs)]
        dqt_ref[...] = jnp.zeros_like(dqt_ref)

        def grad_step(i, _):
            key0 = pl.multiple_of(i * TILE, TILE)
            slot = i - tile_low
            value = kv_ref[pl.ds(key0, TILE), HD:]
            key_t = kt_ref[i]
            for p in range(pairs):
                part = slice(p * pair, (p + 1) * pair)
                dp = lax.dot_general(value, do_rows[part, :], LAST, preferred_element_type=jnp.float32)
                ds_ref[:, part] = (e_ref[slot, :, part].astype(jnp.float32) * (dp - delta[p])).astype(jnp.bfloat16)
            dv_acc[pl.ds(key0, TILE), :] += jnp.dot(e_ref[slot], do_over[...], preferred_element_type=jnp.float32)
            dk_acc[pl.ds(key0, TILE), :] += jnp.dot(ds_ref[...], q_over[...], preferred_element_type=jnp.float32)
            dqt_ref[...] += jnp.dot(key_t, ds_ref[...], preferred_element_type=jnp.float32)
            return 0

        lax.fori_loop(tile_low, tile_end, grad_step, 0)
        for h in range(heads):
            part = slice(h * CHUNK, (h + 1) * CHUNK)
            dq_ref[pl.ds(t0, CHUNK), h * HD:(h + 1) * HD] = (
                dqt_ref[:, part] * (stat_ref[:, part] * scale)).T.astype(jnp.bfloat16)
        return 0

    lax.fori_loop(0, chunks, one_chunk, 0)

    def write(i, _):
        at = pl.ds(pl.multiple_of(i * TILE, TILE), TILE)
        dkv_ref[at, :HD] = (dk_acc[at, :] * scale).astype(jnp.bfloat16)
        dkv_ref[at, HD:] = dv_acc[at, :].astype(jnp.bfloat16)
        return 0

    lax.fori_loop(0, tiles, write, 0)


def attention(starts, lengths, q, do, delta, kv, longest=4608):
    total = kv.shape[0]
    rows = q.shape[1] // HD * CHUNK
    max_tiles = (longest + CHUNK) // TILE + 2
    vmem = pl.BlockSpec(memory_space=pltpu.VMEM)
    smem = pl.BlockSpec(memory_space=pltpu.SMEM)
    return pl.pallas_call(
        functools.partial(attention_kernel, total),
        out_shape=[jax.ShapeDtypeStruct(q.shape, jnp.bfloat16),
                   jax.ShapeDtypeStruct(kv.shape, jnp.bfloat16)],
        in_specs=[smem, smem] + [vmem] * 4,
        out_specs=[vmem] * 2,
        scratch_shapes=[
            pltpu.VMEM((max_tiles, TILE, rows), jnp.bfloat16),
            pltpu.VMEM((TILE, rows), jnp.bfloat16),
            pltpu.VMEM((max_tiles, 1, rows), jnp.float32),
            pltpu.VMEM((rows, HD), jnp.bfloat16),
            pltpu.VMEM((rows, HD), jnp.bfloat16),
            pltpu.VMEM((rows, HD), jnp.bfloat16),
            pltpu.VMEM((rows, HD), jnp.bfloat16),
            pltpu.VMEM((total // TILE, HD, TILE), jnp.bfloat16),
            pltpu.VMEM((HD, rows), jnp.float32),
            pltpu.VMEM((total, HD), jnp.float32),
            pltpu.VMEM((total, HD), jnp.float32),
            pltpu.VMEM((1, rows), jnp.float32),
        ],
        compiler_params=pltpu.CompilerParams(vmem_limit_bytes=60 * 2**20),
        name="attention",
    )(starts, lengths, q, do, delta, kv)


SIDE = 4
MESH = pl.DeviceIdType.MESH


def ring_place(axis, step):
    me = lax.axis_index("ctx")
    x, z = me // SIDE, me % SIDE
    if axis == 0:
        return lax.rem(x + step + SIDE, SIDE) * SIDE + z
    return x * SIDE + lax.rem(z + step + SIDE, SIDE)


def block_at(axis, first, second):
    me = lax.axis_index("ctx")
    x, z = me // SIDE, me % SIDE
    along, across = (first, second) if axis == 0 else (second, first)
    return lax.rem(x + along + SIDE, SIDE) * SIDE + lax.rem(z + across + SIDE, SIDE)


def greet(partners):
    barrier = pltpu.get_barrier_semaphore()
    for partner in partners:
        pl.semaphore_signal(barrier, inc=1, device_id=partner, device_id_type=MESH)
    pl.semaphore_wait(barrier, len(partners))


def collect_kernel(k_ref, v_ref, out_grad_ref, outputs_ref, kv_ref, delta_ref, local_sem, send_sem, recv_sem):
    me = lax.axis_index("ctx")
    rows = k_ref.shape[0]
    half = rows // 2
    quarter = half // 2
    own = [
        pltpu.make_async_copy(k_ref, kv_ref.at[me, :, pl.ds(0, HD)], local_sem.at[0]),
        pltpu.make_async_copy(v_ref, kv_ref.at[me, :, pl.ds(HD, HD)], local_sem.at[1]),
    ]
    for copy in own:
        copy.start()
    greet([{"ctx": ring_place(axis, step)} for axis in (0, 1) for step in (1, -1)])
    for copy in own:
        copy.wait()
    copies = {}

    def begin(name, number, axis, step, block, start, count):
        region = kv_ref.at[block, pl.ds(start, count), :]
        copy = pltpu.make_async_remote_copy(
            src_ref=region, dst_ref=region, send_sem=send_sem.at[number], recv_sem=recv_sem.at[number],
            device_id={"ctx": ring_place(axis, step)}, device_id_type=MESH)
        copy.start()
        copies[name] = copy

    def near(h, item, shift):
        axis = h if item == "line" else 1 - h
        base = h * 20 + (0 if item == "line" else 4 + 4 * item)
        block = me if item == "line" else block_at(h, shift, 0)
        begin((h, item, 0), base, axis, 1, block, h * half, half)
        begin((h, item, 1), base + 1, axis, -1, block, h * half, half)

    def far(h, item, shift):
        axis = h if item == "line" else 1 - h
        base = h * 20 + (0 if item == "line" else 4 + 4 * item)

        def block(step):
            return block_at(h, step, 0) if item == "line" else block_at(h, shift, step)

        copies[h, item, 0].wait_recv()
        begin((h, item, 2), base + 2, axis, 1, block(-1), h * half, quarter)
        copies[h, item, 1].wait_recv()
        begin((h, item, 3), base + 3, axis, -1, block(1), h * half + quarter, quarter)

    shifts = (0, -1, 1, 2)
    for h in (0, 1):
        near(h, "line", 0)
    for h in (0, 1):
        near(h, 0, shifts[0])
    for head in range(delta_ref.shape[0]):
        part = slice(head * HD, (head + 1) * HD)
        product = out_grad_ref[:, part].astype(jnp.float32) * outputs_ref[:, part].astype(jnp.float32)
        delta_ref[head:head + 1, :] = jnp.sum(product.T, axis=0, keepdims=True)
    for h in (0, 1):
        far(h, "line", 0)
        near(h, 1, shifts[1])
        near(h, 2, shifts[2])
    for h in (0, 1):
        far(h, 0, shifts[0])
    for h in (0, 1):
        copies[h, "line", 2].wait_recv()
        copies[h, "line", 3].wait_recv()
        near(h, 3, shifts[3])
    for item in (1, 2, 3):
        for h in (0, 1):
            far(h, item, shifts[item])
    for item in (0, 1, 2, 3):
        for h in (0, 1):
            copies[h, item, 2].wait_recv()
            copies[h, item, 3].wait_recv()
    for copy in copies.values():
        copy.wait_send()


def collect(keys, values, out_grad, outputs):
    rows = keys.shape[0]
    heads = out_grad.shape[1] // HD
    vmem = pl.BlockSpec(memory_space=pltpu.VMEM)
    anywhere = pl.BlockSpec(memory_space=pl.ANY)
    return pl.pallas_call(
        collect_kernel,
        out_shape=[jax.ShapeDtypeStruct((SIDE * SIDE, rows, 2 * HD), jnp.bfloat16),
                   jax.ShapeDtypeStruct((heads, rows), jnp.float32)],
        in_specs=[anywhere, anywhere, vmem, vmem],
        out_specs=[anywhere, vmem],
        scratch_shapes=[pltpu.SemaphoreType.DMA((2,)), pltpu.SemaphoreType.DMA((40,)), pltpu.SemaphoreType.DMA((40,))],
        compiler_params=pltpu.CompilerParams(collective_id=0, has_side_effects=True, vmem_limit_bytes=32 * 2**20),
        name="collect",
    )(keys, values, out_grad, outputs)


PARTS = 2
RS_ORDER = (2, -1, 1, 0)


def tp_place(step, core):
    y = lax.axis_index("tp") // 2
    return lax.rem(y + step + SIDE, SIDE) * 2 + core


def finish_kernel(dq_ref, dkv_hbm, wq_hbm, wk_hbm, wv_hbm, out_ref, dkv_ref, wq_ref, wkv_ref, acc_ref, sum_ref,
                  low_ref, high_ref, stage_ref, fin_ref, res_ref, pair_out, pair_in, y_stage, y_low, y_high, y_fin,
                  load_sem, send_sem, recv_sem):
    core = lax.axis_index("tp") % 2
    rows = dq_ref.shape[0]
    half = rows // 2
    size = half // PARTS
    mid = size // 2
    loads = [
        pltpu.make_async_copy(dkv_hbm, dkv_ref, load_sem.at[0]),
        pltpu.make_async_copy(wq_hbm, wq_ref, load_sem.at[1]),
        pltpu.make_async_copy(wk_hbm, wkv_ref.at[:, :, pl.ds(0, HD)], load_sem.at[2]),
        pltpu.make_async_copy(wv_hbm, wkv_ref.at[:, :, pl.ds(HD, HD)], load_sem.at[3]),
    ]
    for copy in loads:
        copy.start()
    greet([{"ctx": ring_place(axis, step)} for axis in (0, 1) for step in (1, -1)]
          + [{"tp": tp_place(step, core)} for step in (1, -1)] + [{"tp": tp_place(0, 1 - core)}])
    copies = {}

    def begin(name, number, device, src, dst):
        copy = pltpu.make_async_remote_copy(src_ref=src, dst_ref=dst, send_sem=send_sem.at[number],
                                            recv_sem=recv_sem.at[number], device_id=device, device_id_type=MESH)
        copy.start()
        copies[name] = copy

    def wide(value):
        return value.astype(jnp.float32)

    def ident(s, h, k):
        return (s * 2 + h) * 5 + (4 if k is None else RS_ORDER.index(k))

    def term(s, h, k, shift, start, count):
        if k is None:
            return res_ref.at[s, h, RS_ORDER.index(shift), pl.ds(start, count), :]
        return dkv_ref.at[block_at(h, k, shift), pl.ds(h * half + s * size + start, count), :]

    def ring_axis(h, k):
        return h if k is None else 1 - h

    def reduce_send(s, h, k):
        n, axis = ident(s, h, k), ring_axis(h, k)
        begin(("low", n), 4 * n, {"ctx": ring_place(axis, 1)}, term(s, h, k, 2, 0, mid), low_ref.at[n])
        begin(("high", n), 4 * n + 1, {"ctx": ring_place(axis, -1)}, term(s, h, k, 2, mid, mid), high_ref.at[n])

    def reduce_pass(s, h, k):
        n, axis = ident(s, h, k), ring_axis(h, k)
        copies["low", n].wait_recv()
        stage_ref[n, 0, :mid, :] = (wide(term(s, h, k, 1, 0, mid)[...]) + wide(low_ref[n])).astype(jnp.bfloat16)
        stage_ref[n, 0, mid:, :] = term(s, h, k, 1, mid, mid)[...]
        begin(("up", n), 4 * n + 2, {"ctx": ring_place(axis, 1)}, stage_ref.at[n, 0], fin_ref.at[n, 0])
        copies["high", n].wait_recv()
        stage_ref[n, 1, :mid, :] = term(s, h, k, -1, 0, mid)[...]
        stage_ref[n, 1, mid:, :] = (wide(term(s, h, k, -1, mid, mid)[...]) + wide(high_ref[n])).astype(jnp.bfloat16)
        begin(("down", n), 4 * n + 3, {"ctx": ring_place(axis, -1)}, stage_ref.at[n, 1], fin_ref.at[n, 1])

    def reduce_end(s, h, k):
        n = ident(s, h, k)
        copies["up", n].wait_recv()
        copies["down", n].wait_recv()
        total = wide(term(s, h, k, 0, 0, size)[...]) + wide(fin_ref[n, 0]) + wide(fin_ref[n, 1])
        if k is None:
            sum_ref[pl.ds(h * half + s * size, size), :] = total.astype(jnp.bfloat16)
        else:
            res_ref[s, h, RS_ORDER.index(k)] = total.astype(jnp.bfloat16)

    def reduce_steps(s):
        for k in RS_ORDER:
            for h in (0, 1):
                reduce_send(s, h, k)
        yield
        for k in RS_ORDER:
            for h in (0, 1):
                reduce_pass(s, h, k)
        yield
        for h in (0, 1):
            reduce_end(s, h, 2)
            reduce_send(s, h, None)
        yield
        for h in (0, 1):
            reduce_end(s, h, -1)
            reduce_end(s, h, 1)
        for h in (0, 1):
            reduce_pass(s, h, None)
        yield
        for h in (0, 1):
            reduce_end(s, h, 0)
        yield
        for h in (0, 1):
            reduce_end(s, h, None)
        yield

    def project(g):
        acc_ref[g] = lax.dot_general(dq_ref[...], wq_ref[g], LAST, preferred_element_type=jnp.float32)

    far = 40 * PARTS

    def rows_of(s, h):
        return pl.ds(h * half + s * size, size)

    def spread(s, step):
        n = s * 4 + RS_ORDER.index(step)
        other, mine = tp_place(step, 1 - core), tp_place(step, core)
        for h in (0, 1):
            low = sum_ref[rows_of(s, h), :]
            pair_out[n, h] = (acc_ref[other, rows_of(s, h), :] + lax.dot_general(
                low, wkv_ref[other], LAST, preferred_element_type=jnp.float32)).astype(jnp.bfloat16)
        begin(("pair", n), far + n, {"tp": tp_place(0, 1 - core)}, pair_out.at[n], pair_in.at[n])
        for h in (0, 1):
            low = sum_ref[rows_of(s, h), :]
            acc_ref[mine, rows_of(s, h), :] += lax.dot_general(
                low, wkv_ref[mine], LAST, preferred_element_type=jnp.float32)

    def chip_sum(s, step, h):
        n = s * 4 + RS_ORDER.index(step)
        return acc_ref[tp_place(step, core), rows_of(s, h), :] + wide(pair_in[n, h])

    def y_send(s):
        copies["pair", s * 4].wait_recv()
        for h in (0, 1):
            y_stage[s, 0, h] = chip_sum(s, 2, h).astype(jnp.bfloat16)
        number = far + 4 * PARTS + 4 * s
        begin(("y_low", s), number, {"tp": tp_place(1, core)}, y_stage.at[s, 0, 0], y_low.at[s])
        begin(("y_high", s), number + 1, {"tp": tp_place(-1, core)}, y_stage.at[s, 0, 1], y_high.at[s])

    def y_pass(s, step):
        number = far + 4 * PARTS + 4 * s
        copies["pair", s * 4 + RS_ORDER.index(step)].wait_recv()
        slot, low = (1, 0) if step == 1 else (2, 1)
        y_stage[s, slot, 1 - low] = chip_sum(s, step, 1 - low).astype(jnp.bfloat16)
        copies["y_low" if step == 1 else "y_high", s].wait_recv()
        came = y_low if step == 1 else y_high
        y_stage[s, slot, low] = (chip_sum(s, step, low) + wide(came[s])).astype(jnp.bfloat16)
        begin(("y_fin", s, step), number + 1 + slot, {"tp": tp_place(step, core)}, y_stage.at[s, slot],
              y_fin.at[s, slot - 1])

    def y_end(s):
        copies["pair", s * 4 + 3].wait_recv()
        copies["y_fin", s, 1].wait_recv()
        copies["y_fin", s, -1].wait_recv()
        for h in (0, 1):
            out_ref[rows_of(s, h), :] = (
                chip_sum(s, 0, h) + wide(y_fin[s, 0, h]) + wide(y_fin[s, 1, h])).astype(jnp.bfloat16)

    for copy in loads[:1]:
        copy.wait()
    first, second = reduce_steps(0), reduce_steps(1)
    next(first)
    loads[1].wait()
    for g in (0, 1):
        project(g)
    next(first)
    next(second)
    for g in (2, 3):
        project(g)
    next(first)
    project(4)
    next(first)
    project(5)
    next(first)
    for g in (6, 7):
        project(g)
    loads[2].wait()
    loads[3].wait()
    next(first)
    spread(0, 2)
    next(second)
    spread(0, 1)
    y_send(0)
    spread(0, -1)
    next(second)
    spread(0, 0)
    y_pass(0, 1)
    y_pass(0, -1)
    next(second)
    next(second)
    next(second)
    spread(1, 2)
    spread(1, 1)
    y_send(1)
    spread(1, -1)
    spread(1, 0)
    y_end(0)
    y_pass(1, 1)
    y_pass(1, -1)
    y_end(1)
    for copy in copies.values():
        copy.wait_send()


def finish(query_grad, terms, w_query, w_key, w_value):
    rows = query_grad.shape[0]
    blocks = SIDE * 2
    columns = w_query.shape[0] // blocks
    size = rows // 2 // PARTS
    mid = size // 2
    reduces = 10 * PARTS
    sems = 4 * reduces + 8 * PARTS
    bf = jnp.bfloat16
    vmem = pl.BlockSpec(memory_space=pltpu.VMEM)
    anywhere = pl.BlockSpec(memory_space=pl.ANY)
    return pl.pallas_call(
        finish_kernel,
        out_shape=jax.ShapeDtypeStruct((rows, columns), bf),
        in_specs=[vmem] + [anywhere] * 4,
        out_specs=vmem,
        scratch_shapes=[
            pltpu.VMEM(terms.shape, bf),
            pltpu.VMEM((blocks, columns, w_query.shape[1]), bf),
            pltpu.VMEM((blocks, columns, 2 * HD), bf),
            pltpu.VMEM((blocks, rows, columns), jnp.float32),
            pltpu.VMEM((rows, 2 * HD), bf),
            pltpu.VMEM((reduces, mid, 2 * HD), bf),
            pltpu.VMEM((reduces, mid, 2 * HD), bf),
            pltpu.VMEM((reduces, 2, size, 2 * HD), bf),
            pltpu.VMEM((reduces, 2, size, 2 * HD), bf),
            pltpu.VMEM((PARTS, 2, 4, size, 2 * HD), bf),
            pltpu.VMEM((4 * PARTS, 2, size, columns), bf),
            pltpu.VMEM((4 * PARTS, 2, size, columns), bf),
            pltpu.VMEM((PARTS, 3, 2, size, columns), bf),
            pltpu.VMEM((PARTS, size, columns), bf),
            pltpu.VMEM((PARTS, size, columns), bf),
            pltpu.VMEM((PARTS, 2, 2, size, columns), bf),
            pltpu.SemaphoreType.DMA((4,)),
            pltpu.SemaphoreType.DMA((sems,)),
            pltpu.SemaphoreType.DMA((sems,)),
        ],
        compiler_params=pltpu.CompilerParams(collective_id=1, has_side_effects=True, vmem_limit_bytes=60 * 2**20),
        name="finish",
    )(query_grad, terms, w_query.reshape(blocks, columns, -1), w_key.reshape(blocks, columns, -1),
      w_value.reshape(blocks, columns, -1))


def shards(queries, keys, values, outputs, out_grad, lengths, w_query, w_key, w_value):
    rows = queries.shape[0]
    me = lax.axis_index("ctx")
    starts = me * rows + jnp.arange(rows // CHUNK, dtype=jnp.int32) * CHUNK
    collected, delta = collect(keys, values, out_grad, outputs)
    query_grad, terms = attention(starts, lengths, queries, out_grad, delta, collected.reshape(-1, 2 * HD))
    return finish(query_grad, terms.reshape(collected.shape), w_query, w_key, w_value)


def solution(mesh):
    in_specs = (P("ctx", "tp"),) * 5 + (P(),) + (P(None, "tp"),) * 3
    return jax.shard_map(shards, mesh=mesh, in_specs=in_specs, out_specs=P("ctx", "tp"), check_vma=False)
```

```python
import functools
import jax, jax.numpy as jnp
from jax import lax
from jax.experimental import pallas as pl
from jax.experimental.pallas import tpu as pltpu
from jax.sharding import PartitionSpec as P

HD = 128
CHUNK = 128
TILE = 256
NEG = -1e30
SAFE = 60.0
LAST = (((1,), (1,)), ((), ()))


PIECES = 4


def attention_kernel(total, start_ref, lengths_ref, row_ref, q_hbm, do_hbm, kv_hbm,
                     dq_hbm, dkv_hbm, q_ref, do_ref, kv_ref, dq_ref, dkv_ref, load_sem, store_sem, e_ref, ds_ref, mt_ref, q_rows, do_rows, q_over, do_over, kt_ref, dqt_ref,
                     dk_acc, dv_acc, stat_ref):
    rows = q_rows.shape[0]
    heads = rows // CHUNK
    pair = 2 * CHUNK
    pairs = rows // pair
    chunks = q_ref.shape[0] // CHUNK
    tiles = total // TILE
    scale = HD ** -0.5
    to_log2 = scale * 1.4426950408889634

    piece = total // PIECES
    loads = [pltpu.make_async_copy(kv_hbm.at[pl.ds(n * piece, piece), :], kv_ref.at[pl.ds(n * piece, piece), :],
                                   load_sem.at[n]) for n in range(PIECES)]
    loads += [pltpu.make_async_copy(q_hbm, q_ref, load_sem.at[PIECES]),
              pltpu.make_async_copy(do_hbm, do_ref, load_sem.at[PIECES + 1])]
    for copy in loads:
        copy.start()

    def clear(i, _):
        at = pl.ds(pl.multiple_of(i * TILE, TILE), TILE)
        dk_acc[at, :] = jnp.zeros((TILE, HD), jnp.float32)
        dv_acc[at, :] = jnp.zeros((TILE, HD), jnp.float32)
        return 0

    lax.fori_loop(0, tiles, clear, 0)

    def turn_keys(i, most):
        turned = kv_ref[pl.ds(pl.multiple_of(i * TILE, TILE), TILE), :HD].T
        kt_ref[i] = turned
        wide = turned.astype(jnp.float32)
        return jnp.maximum(most, jnp.sum(wide * wide, axis=0, keepdims=True))

    key_most = jnp.zeros((1, TILE), jnp.float32)
    for n in range(PIECES):
        loads[n].wait()
        key_most = lax.fori_loop(n * tiles // PIECES, (n + 1) * tiles // PIECES, turn_keys, key_most, unroll=4)
    key_most = jnp.max(key_most)
    for copy in loads[PIECES:]:
        copy.wait()

    def one_chunk(j, _):
        first = start_ref[j]
        t0 = pl.multiple_of(j * CHUNK, CHUNK)
        for h in range(heads):
            part = q_ref[pl.ds(t0, CHUNK), h * HD:(h + 1) * HD]
            q_rows[h * CHUNK:(h + 1) * CHUNK, :] = part
            do_rows[h * CHUNK:(h + 1) * CHUNK, :] = do_ref[pl.ds(t0, CHUNK), h * HD:(h + 1) * HD]
        small = jnp.max(row_ref[heads:, pl.ds(t0, CHUNK)]) * key_most * (to_log2 * to_log2) <= SAFE * SAFE
        query_pos = first + lax.broadcasted_iota(jnp.int32, (1, pair), 1) % CHUNK
        row_start = jnp.zeros((1, pair), jnp.int32)
        low, high = jnp.int32(0), jnp.int32(0)
        begin = jnp.int32(0)
        for d in range(lengths_ref.shape[0]):
            row_start = jnp.where(query_pos >= begin, begin, row_start)
            low = jnp.where(first >= begin, begin, low)
            high = jnp.where(first + CHUNK - 1 >= begin, begin, high)
            begin = begin + lengths_ref[d]
        tile_low = low // TILE
        tile_end = (first + CHUNK - 1) // TILE + 1
        plain_low = jnp.minimum((high + TILE - 1) // TILE, tile_end)
        plain_end = jnp.maximum((first + 1) // TILE, plain_low)
        edge = plain_low - tile_low
        edges = edge + tile_end - plain_end

        def edge_tile(n):
            return jnp.where(n < edge, tile_low + n, plain_end + n - edge)

        def allowed_of(key0):
            key_pos = key0 + lax.broadcasted_iota(jnp.int32, (TILE, pair), 0)
            return (key_pos >= row_start) & (key_pos <= query_pos)

        def scores(key, p):
            return lax.dot_general(key, q_rows[p * pair:(p + 1) * pair, :], LAST,
                                   preferred_element_type=jnp.float32) * to_log2

        def weigh(i, sums, masked):
            key0 = pl.multiple_of(i * TILE, TILE)
            key = kv_ref[pl.ds(key0, TILE), :HD]
            new = []
            for p in range(pairs):
                e = jnp.exp2(scores(key, p))
                if masked:
                    e = jnp.where(allowed_of(key0), e, 0.0)
                new.append(sums[p] + jnp.sum(e.reshape(TILE // 8, 8, pair), axis=0))
                e_ref[i - tile_low, :, p * pair:(p + 1) * pair] = e.astype(jnp.bfloat16)
            return tuple(new)

        @pl.when(small)
        def _():
            sums = tuple(jnp.zeros((8, pair), jnp.float32) for _ in range(pairs))
            sums = lax.fori_loop(0, edges, lambda n, s: weigh(edge_tile(n), s, True), sums)
            sums = lax.fori_loop(plain_low, plain_end, lambda i, s: weigh(i, s, False), sums)
            for p in range(pairs):
                stat_ref[:, p * pair:(p + 1) * pair] = 1.0 / jnp.sum(sums[p], axis=0, keepdims=True)

        @pl.when(jnp.logical_not(small))
        def _():
            def step(i, carry):
                tops, sums = carry
                key0 = pl.multiple_of(i * TILE, TILE)
                key = kv_ref[pl.ds(key0, TILE), :HD]
                new_tops, new_sums = [], []
                for p in range(pairs):
                    s = jnp.where(allowed_of(key0), scores(key, p), NEG)
                    top = jnp.maximum(tops[p], jnp.max(s, axis=0, keepdims=True))
                    e = jnp.exp2(s - top)
                    new_sums.append(sums[p] * jnp.exp2(tops[p] - top) + jnp.sum(e, axis=0, keepdims=True))
                    new_tops.append(top)
                    e_ref[i - tile_low, :, p * pair:(p + 1) * pair] = e.astype(jnp.bfloat16)
                    mt_ref[i - tile_low, :, p * pair:(p + 1) * pair] = top
                return tuple(new_tops), tuple(new_sums)

            tops, sums = lax.fori_loop(tile_low, tile_end, step, (
                tuple(jnp.full((1, pair), NEG, jnp.float32) for _ in range(pairs)),
                tuple(jnp.zeros((1, pair), jnp.float32) for _ in range(pairs))))

            def settle(i, _):
                for p in range(pairs):
                    part = slice(p * pair, (p + 1) * pair)
                    factor = jnp.exp2(mt_ref[i - tile_low, :, part] - tops[p])
                    e_ref[i - tile_low, :, part] = (
                        e_ref[i - tile_low, :, part].astype(jnp.float32) * factor).astype(jnp.bfloat16)
                return 0

            lax.fori_loop(tile_low, tile_end, settle, 0)
            for p in range(pairs):
                stat_ref[:, p * pair:(p + 1) * pair] = 1.0 / sums[p]

        for h in range(heads):
            part = slice(h * CHUNK, (h + 1) * CHUNK)
            inverse = jnp.broadcast_to(stat_ref[:, part], (HD, CHUNK)).T
            q_over[part, :] = (q_rows[part, :].astype(jnp.float32) * inverse).astype(jnp.bfloat16)
            do_over[part, :] = (do_rows[part, :].astype(jnp.float32) * inverse).astype(jnp.bfloat16)
        delta = [jnp.concatenate([row_ref[2 * p:2 * p + 1, pl.ds(t0, CHUNK)],
                                  row_ref[2 * p + 1:2 * p + 2, pl.ds(t0, CHUNK)]], axis=1) for p in range(pairs)]
        dqt_ref[...] = jnp.zeros_like(dqt_ref)

        def grad_step(i, _):
            key0 = pl.multiple_of(i * TILE, TILE)
            slot = i - tile_low
            value = kv_ref[pl.ds(key0, TILE), HD:]
            key_t = kt_ref[i]
            for p in range(pairs):
                part = slice(p * pair, (p + 1) * pair)
                dp = lax.dot_general(value, do_rows[part, :], LAST, preferred_element_type=jnp.float32)
                ds_ref[:, part] = (e_ref[slot, :, part].astype(jnp.float32) * (dp - delta[p])).astype(jnp.bfloat16)
            dv_acc[pl.ds(key0, TILE), :] += jnp.dot(e_ref[slot], do_over[...], preferred_element_type=jnp.float32)
            dk_acc[pl.ds(key0, TILE), :] += jnp.dot(ds_ref[...], q_over[...], preferred_element_type=jnp.float32)
            dqt_ref[...] += jnp.dot(key_t, ds_ref[...], preferred_element_type=jnp.float32)
            return 0

        lax.fori_loop(tile_low, tile_end, grad_step, 0)
        for h in range(heads):
            part = slice(h * CHUNK, (h + 1) * CHUNK)
            dq_ref[pl.ds(t0, CHUNK), h * HD:(h + 1) * HD] = (
                dqt_ref[:, part] * (stat_ref[:, part] * scale)).T.astype(jnp.bfloat16)
        pltpu.make_async_copy(dq_ref.at[pl.ds(t0, CHUNK), :], dq_hbm.at[pl.ds(t0, CHUNK), :], store_sem.at[j]).start()
        return 0

    lax.fori_loop(0, chunks, one_chunk, 0)

    def write(i, _):
        at = pl.ds(pl.multiple_of(i * TILE, TILE), TILE)
        dkv_ref[at, :HD] = (dk_acc[at, :] * scale).astype(jnp.bfloat16)
        dkv_ref[at, HD:] = dv_acc[at, :].astype(jnp.bfloat16)
        return 0

    stores = []
    for n in range(PIECES):
        lax.fori_loop(n * tiles // PIECES, (n + 1) * tiles // PIECES, write, 0)
        stores.append(pltpu.make_async_copy(dkv_ref.at[pl.ds(n * piece, piece), :],
                                            dkv_hbm.at[pl.ds(n * piece, piece), :], store_sem.at[chunks + n]))
        stores[-1].start()
    for j in range(chunks):
        part = pl.ds(j * CHUNK, CHUNK)
        pltpu.make_async_copy(dq_ref.at[part, :], dq_hbm.at[part, :], store_sem.at[j]).wait()
    for copy in stores:
        copy.wait()


def attention(starts, lengths, q, do, row_info, kv, longest=4608):
    total = kv.shape[0]
    rows = q.shape[1] // HD * CHUNK
    max_tiles = (longest + CHUNK) // TILE + 2
    vmem = pl.BlockSpec(memory_space=pltpu.VMEM)
    smem = pl.BlockSpec(memory_space=pltpu.SMEM)
    anywhere = pl.BlockSpec(memory_space=pl.ANY)
    return pl.pallas_call(
        functools.partial(attention_kernel, total),
        out_shape=[jax.ShapeDtypeStruct(q.shape, jnp.bfloat16),
                   jax.ShapeDtypeStruct(kv.shape, jnp.bfloat16)],
        in_specs=[smem, smem, vmem] + [anywhere] * 3,
        out_specs=[anywhere] * 2,
        scratch_shapes=[
            pltpu.VMEM(q.shape, jnp.bfloat16),
            pltpu.VMEM(q.shape, jnp.bfloat16),
            pltpu.VMEM(kv.shape, jnp.bfloat16),
            pltpu.VMEM(q.shape, jnp.bfloat16),
            pltpu.VMEM(kv.shape, jnp.bfloat16),
            pltpu.SemaphoreType.DMA((PIECES + 2,)),
            pltpu.SemaphoreType.DMA((q.shape[0] // CHUNK + PIECES,)),
            pltpu.VMEM((max_tiles, TILE, rows), jnp.bfloat16),
            pltpu.VMEM((TILE, rows), jnp.bfloat16),
            pltpu.VMEM((max_tiles, 1, rows), jnp.float32),
            pltpu.VMEM((rows, HD), jnp.bfloat16),
            pltpu.VMEM((rows, HD), jnp.bfloat16),
            pltpu.VMEM((rows, HD), jnp.bfloat16),
            pltpu.VMEM((rows, HD), jnp.bfloat16),
            pltpu.VMEM((total // TILE, HD, TILE), jnp.bfloat16),
            pltpu.VMEM((HD, rows), jnp.float32),
            pltpu.VMEM((total, HD), jnp.float32),
            pltpu.VMEM((total, HD), jnp.float32),
            pltpu.VMEM((1, rows), jnp.float32),
        ],
        compiler_params=pltpu.CompilerParams(vmem_limit_bytes=62 * 2**20),
        name="attention",
    )(starts, lengths, row_info, q, do, kv)


SIDE = 4
MESH = pl.DeviceIdType.MESH


def ring_place(axis, step):
    me = lax.axis_index("ctx")
    x, z = me // SIDE, me % SIDE
    if axis == 0:
        return lax.rem(x + step + 2 * SIDE, SIDE) * SIDE + z
    return x * SIDE + lax.rem(z + step + SIDE, SIDE)


def block_at(axis, first, second):
    me = lax.axis_index("ctx")
    x, z = me // SIDE, me % SIDE
    along, across = (first, second) if axis == 0 else (second, first)
    return lax.rem(x + along + SIDE, SIDE) * SIDE + lax.rem(z + across + SIDE, SIDE)


def greet(partners):
    barrier = pltpu.get_barrier_semaphore()
    for partner in partners:
        pl.semaphore_signal(barrier, inc=1, device_id=partner, device_id_type=MESH)
    pl.semaphore_wait(barrier, len(partners))


RELAY = ((1, 0), (-1, 1))


def collect_kernel(k_ref, v_ref, q_ref, out_grad_ref, outputs_ref, kv_ref, q_out, out_grad_out, row_out,
                   q_vmem, out_grad_vmem, outputs_vmem, row_vmem, relay, local_sem, send_sem, recv_sem):
    me = lax.axis_index("ctx")
    rows = k_ref.shape[0]
    half = rows // 2
    mid = half // 2
    quarter = rows // SIDE
    own = [
        pltpu.make_async_copy(k_ref, kv_ref.at[me, :, pl.ds(0, HD)], local_sem.at[0]),
        pltpu.make_async_copy(v_ref, kv_ref.at[me, :, pl.ds(HD, HD)], local_sem.at[1]),
    ]
    kept = [
        pltpu.make_async_copy(q_ref, q_vmem, local_sem.at[2]),
        pltpu.make_async_copy(out_grad_ref, out_grad_vmem, local_sem.at[3]),
        pltpu.make_async_copy(outputs_ref, outputs_vmem, local_sem.at[4]),
    ]
    for copy in own + kept:
        copy.start()
    greet([{"ctx": ring_place(axis, step)} for axis, step in ((0, 1), (0, -1), (0, 2), (1, 1), (1, -1))])
    for copy in own:
        copy.wait()
    copies = {}

    def begin(name, number, place, src, dst):
        copy = pltpu.make_async_remote_copy(
            src_ref=src, dst_ref=dst, send_sem=send_sem.at[number], recv_sem=recv_sem.at[number],
            device_id={"ctx": ring_place(*place)}, device_id_type=MESH)
        copy.start()
        copies[name] = copy

    def pass_on(name, number, place, block, start, count):
        region = kv_ref.at[block, pl.ds(start, count), :]
        begin(name, number, place, region, region)

    def near(h, item, shift):
        axis = 0 if item == "line" else 1
        base = h * 20 + (0 if item == "line" else 4 + 4 * item)
        block = me if item == "line" else block_at(0, shift, 0)
        pass_on((h, item, 0), base, (axis, 1), block, h * half, half)
        pass_on((h, item, 1), base + 1, (axis, -1), block, h * half, half)

    def far(h, item, shift):
        axis = 0 if item == "line" else 1
        base = h * 20 + (0 if item == "line" else 4 + 4 * item)

        def block(step):
            return block_at(0, step, 0) if item == "line" else block_at(0, shift, step)

        copies[h, item, 0].wait_recv()
        pass_on((h, item, 2), base + 2, (axis, 1), block(-1), h * half, mid)
        copies[h, item, 1].wait_recv()
        pass_on((h, item, 3), base + 3, (axis, -1), block(1), h * half + mid, mid)

    shifts = (0, -1, 1, 2)
    pairs = ((q_ref, q_out), (out_grad_ref, out_grad_out))
    for h in (0, 1):
        near(h, "line", 0)
    for h in (0, 1):
        near(h, 0, shifts[0])
    for n, (src, dst) in enumerate(pairs):
        for step, slot in RELAY:
            part = pl.ds(2 * quarter + slot * (quarter // 2), quarter // 2)
            begin(("relay", n, slot), 40 + 2 * n + slot, (0, step), src.at[part, :], relay.at[n, slot])
    for n, (src, dst) in enumerate(pairs):
        for j, step in ((1, 1), (3, -1)):
            part = pl.ds(j * quarter, quarter)
            begin(("move", n, j), 44 + 2 * n + j // 2, (0, step), src.at[part, :], dst.at[part, :])
    for copy in kept:
        copy.wait()
    stay = [
        pltpu.make_async_copy(q_vmem.at[pl.ds(0, quarter), :], q_out.at[pl.ds(0, quarter), :], local_sem.at[0]),
        pltpu.make_async_copy(out_grad_vmem.at[pl.ds(0, quarter), :], out_grad_out.at[pl.ds(0, quarter), :],
                              local_sem.at[1]),
    ]
    for copy in stay:
        copy.start()
    heads = row_vmem.shape[0] // 2
    for head in range(heads):
        part = slice(head * HD, (head + 1) * HD)
        grad = out_grad_vmem[:, part].astype(jnp.float32)
        query = q_vmem[:, part].astype(jnp.float32)
        row_vmem[head:head + 1, :] = jnp.sum((grad * outputs_vmem[:, part].astype(jnp.float32)).T, axis=0, keepdims=True)
        row_vmem[heads + head:heads + head + 1, :] = jnp.sum((query * query).T, axis=0, keepdims=True)
    for j, step in ((1, 1), (2, 2), (3, -1)):
        part = pl.ds(j * quarter, quarter)
        begin(("rows", j), 51 + j, (0, step), row_vmem.at[:, part], row_out.at[:, part])
    row_out[:, :quarter] = row_vmem[:, :quarter]
    for h in (0, 1):
        far(h, "line", 0)
        near(h, 1, shifts[1])
        near(h, 2, shifts[2])
    for n, (src, dst) in enumerate(pairs):
        for step, slot in RELAY:
            part = pl.ds(2 * quarter + slot * (quarter // 2), quarter // 2)
            copies["relay", n, slot].wait_recv()
            begin(("relayed", n, slot), 48 + 2 * n + slot, (0, step), relay.at[n, slot], dst.at[part, :])
    for h in (0, 1):
        far(h, 0, shifts[0])
    for h in (0, 1):
        copies[h, "line", 2].wait_recv()
        copies[h, "line", 3].wait_recv()
        near(h, 3, shifts[3])
    for item in (1, 2, 3):
        for h in (0, 1):
            far(h, item, shifts[item])
    for item in (0, 1, 2, 3):
        for h in (0, 1):
            copies[h, item, 2].wait_recv()
            copies[h, item, 3].wait_recv()
    for n in (0, 1):
        for name in (("move", n, 1), ("move", n, 3), ("relayed", n, 0), ("relayed", n, 1)):
            copies[name].wait_recv()
    for j in (1, 2, 3):
        copies["rows", j].wait_recv()
    for copy in stay:
        copy.wait()
    for copy in copies.values():
        copy.wait_send()


def collect(keys, values, queries, out_grad, outputs):
    rows = keys.shape[0]
    heads = out_grad.shape[1] // HD
    bf = jnp.bfloat16
    vmem = pl.BlockSpec(memory_space=pltpu.VMEM)
    anywhere = pl.BlockSpec(memory_space=pl.ANY)
    return pl.pallas_call(
        collect_kernel,
        out_shape=[jax.ShapeDtypeStruct((SIDE * SIDE, rows, 2 * HD), bf),
                   jax.ShapeDtypeStruct(queries.shape, bf),
                   jax.ShapeDtypeStruct(queries.shape, bf),
                   jax.ShapeDtypeStruct((2 * heads, rows), jnp.float32)],
        in_specs=[anywhere] * 5,
        out_specs=[anywhere] * 3 + [vmem],
        scratch_shapes=[pltpu.VMEM(queries.shape, bf), pltpu.VMEM(queries.shape, bf), pltpu.VMEM(queries.shape, bf),
                        pltpu.VMEM((2 * heads, rows), jnp.float32),
                        pltpu.VMEM((2, 2, rows // SIDE // 2, queries.shape[1]), bf),
                        pltpu.SemaphoreType.DMA((5,)), pltpu.SemaphoreType.DMA((55,)), pltpu.SemaphoreType.DMA((55,))],
        compiler_params=pltpu.CompilerParams(collective_id=0, has_side_effects=True, vmem_limit_bytes=62 * 2**20),
        name="collect",
    )(keys, values, queries, out_grad, outputs)


PARTS = 4
PART_ORDER = (0, 1, 3, 2)
FIRST_AXIS = ((0, 0), (0, 0), (0, 1), (0, 1))
RS_ORDER = (2, -1, 1, 0)


def tp_place(step, core):
    y = lax.axis_index("tp") // 2
    return lax.rem(y + step + SIDE, SIDE) * 2 + core


def finish_kernel(dq_hbm, dkv_hbm, wq_hbm, wk_hbm, wv_hbm, out_ref, dq_ref, relay, dkv_ref, wq_ref, wkv_ref, acc_ref, sum_ref,
                  low_ref, high_ref, stage_ref, fin_ref, res_ref, pair_out, pair_in, y_stage, y_low, y_high, y_fin,
                  load_sem, send_sem, recv_sem):
    core = lax.axis_index("tp") % 2
    rows = dq_ref.shape[0]
    part_rows = rows // PARTS
    size = part_rows // 2
    mid = size // 2
    loads = [
        pltpu.make_async_copy(dkv_hbm, dkv_ref, load_sem.at[0]),
        pltpu.make_async_copy(wq_hbm, wq_ref, load_sem.at[1]),
        pltpu.make_async_copy(wk_hbm, wkv_ref.at[:, :, pl.ds(0, HD)], load_sem.at[2]),
        pltpu.make_async_copy(wv_hbm, wkv_ref.at[:, :, pl.ds(HD, HD)], load_sem.at[3]),
        pltpu.make_async_copy(dq_hbm.at[pl.ds(0, part_rows), :], dq_ref.at[pl.ds(0, part_rows), :], load_sem.at[4]),
    ]
    for copy in loads:
        copy.start()
    greet([{"ctx": ring_place(axis, step)} for axis in (0, 1) for step in (1, -1)]
          + [{"tp": tp_place(step, core)} for step in (1, -1)] + [{"tp": tp_place(0, 1 - core)}])
    copies = {}

    def begin(name, number, device, src, dst):
        copy = pltpu.make_async_remote_copy(src_ref=src, dst_ref=dst, send_sem=send_sem.at[number],
                                            recv_sem=recv_sem.at[number], device_id=device, device_id_type=MESH)
        copy.start()
        copies[name] = copy

    def wide(value):
        return value.astype(jnp.float32)

    def rows_of(s, h):
        return pl.ds(s * part_rows + h * size, size)

    def ident(s, h, k):
        return (s * 2 + h) * 5 + (4 if k is None else RS_ORDER.index(k))

    def term(s, h, k, shift, start, count):
        if k is None:
            return res_ref.at[s, h, RS_ORDER.index(shift), pl.ds(start, count), :]
        return dkv_ref.at[block_at(FIRST_AXIS[s][h], k, shift), pl.ds(s * part_rows + h * size + start, count), :]

    def ring_axis(s, h, k):
        return FIRST_AXIS[s][h] if k is None else 1 - FIRST_AXIS[s][h]

    def reduce_send(s, h, k):
        n, axis = ident(s, h, k), ring_axis(s, h, k)
        begin(("low", n), 4 * n, {"ctx": ring_place(axis, 1)}, term(s, h, k, 2, 0, mid), low_ref.at[n])
        begin(("high", n), 4 * n + 1, {"ctx": ring_place(axis, -1)}, term(s, h, k, 2, mid, mid), high_ref.at[n])

    def reduce_pass(s, h, k):
        n, axis = ident(s, h, k), ring_axis(s, h, k)
        copies["low", n].wait_recv()
        stage_ref[n, 0, :mid, :] = (wide(term(s, h, k, 1, 0, mid)[...]) + wide(low_ref[n])).astype(jnp.bfloat16)
        stage_ref[n, 0, mid:, :] = term(s, h, k, 1, mid, mid)[...]
        begin(("up", n), 4 * n + 2, {"ctx": ring_place(axis, 1)}, stage_ref.at[n, 0], fin_ref.at[n, 0])
        copies["high", n].wait_recv()
        stage_ref[n, 1, :mid, :] = term(s, h, k, -1, 0, mid)[...]
        stage_ref[n, 1, mid:, :] = (wide(term(s, h, k, -1, mid, mid)[...]) + wide(high_ref[n])).astype(jnp.bfloat16)
        begin(("down", n), 4 * n + 3, {"ctx": ring_place(axis, -1)}, stage_ref.at[n, 1], fin_ref.at[n, 1])

    def reduce_end(s, h, k):
        n = ident(s, h, k)
        copies["up", n].wait_recv()
        copies["down", n].wait_recv()
        total = wide(term(s, h, k, 0, 0, size)[...]) + wide(fin_ref[n, 0]) + wide(fin_ref[n, 1])
        if k is None:
            sum_ref[rows_of(s, h), :] = total.astype(jnp.bfloat16)
        else:
            res_ref[s, h, RS_ORDER.index(k)] = total.astype(jnp.bfloat16)

    def reduce_steps(s):
        for k in RS_ORDER:
            for h in (0, 1):
                reduce_send(s, h, k)
        yield
        for k in RS_ORDER:
            for h in (0, 1):
                reduce_pass(s, h, k)
        yield
        for h in (0, 1):
            reduce_end(s, h, 2)
            reduce_send(s, h, None)
        yield
        for h in (0, 1):
            reduce_end(s, h, -1)
            reduce_end(s, h, 1)
        for h in (0, 1):
            reduce_pass(s, h, None)
        yield
        for h in (0, 1):
            reduce_end(s, h, 0)
        yield
        for h in (0, 1):
            reduce_end(s, h, None)
        yield

    def project(g, n):
        part = pl.ds(n * (rows // 2), rows // 2)
        acc_ref[g, part, :] = lax.dot_general(dq_ref[part, :], wq_ref[g], LAST, preferred_element_type=jnp.float32)

    back = 48 * PARTS

    def give_back():
        for step, slot in RELAY:
            part = pl.ds(2 * part_rows + slot * size, size)
            begin(("relay", slot), back + slot, {"ctx": ring_place(0, step)}, dq_hbm.at[part, :], relay.at[slot])
        for j, step in ((1, -1), (3, 1)):
            part = pl.ds(j * part_rows, part_rows)
            begin(("back", j), back + 2 + j // 2, {"ctx": ring_place(0, step)}, dq_hbm.at[part, :], dq_ref.at[part, :])

    def relay_back():
        for step, slot in RELAY:
            part = pl.ds(2 * part_rows + slot * size, size)
            copies["relay", slot].wait_recv()
            begin(("relayed", slot), back + 4 + slot, {"ctx": ring_place(0, step)}, relay.at[slot], dq_ref.at[part, :])

    far = 40 * PARTS

    def spread(s, step):
        n = s * 4 + RS_ORDER.index(step)
        other, mine = tp_place(step, 1 - core), tp_place(step, core)
        for h in (0, 1):
            low = sum_ref[rows_of(s, h), :]
            pair_out[n, h] = (acc_ref[other, rows_of(s, h), :] + lax.dot_general(
                low, wkv_ref[other], LAST, preferred_element_type=jnp.float32)).astype(jnp.bfloat16)
        begin(("pair", n), far + n, {"tp": tp_place(0, 1 - core)}, pair_out.at[n], pair_in.at[n])
        for h in (0, 1):
            low = sum_ref[rows_of(s, h), :]
            acc_ref[mine, rows_of(s, h), :] += lax.dot_general(
                low, wkv_ref[mine], LAST, preferred_element_type=jnp.float32)

    def chip_sum(s, step, h):
        n = s * 4 + RS_ORDER.index(step)
        return acc_ref[tp_place(step, core), rows_of(s, h), :] + wide(pair_in[n, h])

    def y_send(s):
        copies["pair", s * 4].wait_recv()
        for h in (0, 1):
            y_stage[s, 0, h] = chip_sum(s, 2, h).astype(jnp.bfloat16)
        number = far + 4 * PARTS + 4 * s
        begin(("y_low", s), number, {"tp": tp_place(1, core)}, y_stage.at[s, 0, 0], y_low.at[s])
        begin(("y_high", s), number + 1, {"tp": tp_place(-1, core)}, y_stage.at[s, 0, 1], y_high.at[s])

    def y_pass(s, step):
        number = far + 4 * PARTS + 4 * s
        copies["pair", s * 4 + RS_ORDER.index(step)].wait_recv()
        slot, low = (1, 0) if step == 1 else (2, 1)
        y_stage[s, slot, 1 - low] = chip_sum(s, step, 1 - low).astype(jnp.bfloat16)
        copies["y_low" if step == 1 else "y_high", s].wait_recv()
        came = y_low if step == 1 else y_high
        y_stage[s, slot, low] = (chip_sum(s, step, low) + wide(came[s])).astype(jnp.bfloat16)
        begin(("y_fin", s, step), number + 1 + slot, {"tp": tp_place(step, core)}, y_stage.at[s, slot],
              y_fin.at[s, slot - 1])

    def y_end(s):
        copies["pair", s * 4 + 3].wait_recv()
        copies["y_fin", s, 1].wait_recv()
        copies["y_fin", s, -1].wait_recv()
        for h in (0, 1):
            out_ref[rows_of(s, h), :] = (
                chip_sum(s, 0, h) + wide(y_fin[s, 0, h]) + wide(y_fin[s, 1, h])).astype(jnp.bfloat16)

    give_back()
    sums = {s: reduce_steps(s) for s in PART_ORDER}
    one, two, three, four = PART_ORDER
    loads[0].wait()
    next(sums[one])
    relay_back()
    next(sums[one])
    next(sums[two])
    copies["back", 1].wait_recv()
    loads[4].wait()
    loads[1].wait()
    for g in range(4):
        project(g, 0)
    next(sums[one])
    next(sums[two])
    next(sums[three])
    for g in range(4, 8):
        project(g, 0)
    next(sums[one])
    next(sums[one])
    next(sums[two])
    loads[2].wait()
    loads[3].wait()
    next(sums[one])
    for step in RS_ORDER:
        spread(one, step)
    next(sums[three])
    next(sums[four])
    next(sums[two])
    y_send(one)
    copies["back", 3].wait_recv()
    copies["relayed", 0].wait_recv()
    copies["relayed", 1].wait_recv()
    for g in range(4):
        project(g, 1)
    next(sums[two])
    y_pass(one, 1)
    y_pass(one, -1)
    next(sums[two])
    next(sums[three])
    for step in RS_ORDER:
        spread(two, step)
    for g in range(4, 8):
        project(g, 1)
    next(sums[three])
    next(sums[four])
    y_send(two)
    next(sums[three])
    next(sums[four])
    y_pass(two, 1)
    y_pass(two, -1)
    next(sums[three])
    for step in RS_ORDER:
        spread(three, step)
    next(sums[four])
    y_send(three)
    next(sums[four])
    next(sums[four])
    for step in RS_ORDER:
        spread(four, step)
    y_pass(three, 1)
    y_pass(three, -1)
    y_send(four)
    y_end(one)
    y_end(two)
    y_pass(four, 1)
    y_pass(four, -1)
    y_end(three)
    y_end(four)
    for copy in copies.values():
        copy.wait_send()


def finish(query_grad, terms, w_query, w_key, w_value):
    rows = query_grad.shape[0]
    blocks = SIDE * 2
    columns = w_query.shape[0] // blocks
    size = rows // PARTS // 2
    mid = size // 2
    reduces = 10 * PARTS
    sems = 4 * reduces + 8 * PARTS + 6
    bf = jnp.bfloat16
    vmem = pl.BlockSpec(memory_space=pltpu.VMEM)
    anywhere = pl.BlockSpec(memory_space=pl.ANY)
    return pl.pallas_call(
        finish_kernel,
        out_shape=jax.ShapeDtypeStruct((rows, columns), bf),
        in_specs=[anywhere] * 5,
        out_specs=vmem,
        scratch_shapes=[
            pltpu.VMEM(query_grad.shape, bf),
            pltpu.VMEM((2, size, query_grad.shape[1]), bf),
            pltpu.VMEM(terms.shape, bf),
            pltpu.VMEM((blocks, columns, w_query.shape[1]), bf),
            pltpu.VMEM((blocks, columns, 2 * HD), bf),
            pltpu.VMEM((blocks, rows, columns), jnp.float32),
            pltpu.VMEM((rows, 2 * HD), bf),
            pltpu.VMEM((reduces, mid, 2 * HD), bf),
            pltpu.VMEM((reduces, mid, 2 * HD), bf),
            pltpu.VMEM((reduces, 2, size, 2 * HD), bf),
            pltpu.VMEM((reduces, 2, size, 2 * HD), bf),
            pltpu.VMEM((PARTS, 2, 4, size, 2 * HD), bf),
            pltpu.VMEM((4 * PARTS, 2, size, columns), bf),
            pltpu.VMEM((4 * PARTS, 2, size, columns), bf),
            pltpu.VMEM((PARTS, 3, 2, size, columns), bf),
            pltpu.VMEM((PARTS, size, columns), bf),
            pltpu.VMEM((PARTS, size, columns), bf),
            pltpu.VMEM((PARTS, 2, 2, size, columns), bf),
            pltpu.SemaphoreType.DMA((5,)),
            pltpu.SemaphoreType.DMA((sems,)),
            pltpu.SemaphoreType.DMA((sems,)),
        ],
        compiler_params=pltpu.CompilerParams(collective_id=1, has_side_effects=True, vmem_limit_bytes=62 * 2**20),
        name="finish",
    )(query_grad, terms, w_query.reshape(blocks, columns, -1), w_key.reshape(blocks, columns, -1),
      w_value.reshape(blocks, columns, -1))


def shards(queries, keys, values, outputs, out_grad, lengths, w_query, w_key, w_value):
    rows = queries.shape[0]
    starts = jnp.stack([ring_place(0, -j) * rows + j * CHUNK for j in range(SIDE)]).astype(jnp.int32)
    collected, q_work, grad_work, row_info = collect(keys, values, queries, out_grad, outputs)
    query_grad, terms = attention(starts, lengths, q_work, grad_work, row_info, collected.reshape(-1, 2 * HD))
    return finish(query_grad, terms.reshape(collected.shape), w_query, w_key, w_value)


def solution(mesh):
    in_specs = (P("ctx", "tp"),) * 5 + (P(),) + (P(None, "tp"),) * 3
    return jax.shard_map(shards, mesh=mesh, in_specs=in_specs, out_specs=P("ctx", "tp"), check_vma=False)
```

```python
import functools
import jax, jax.numpy as jnp
from jax import lax
from jax.experimental import pallas as pl
from jax.experimental.pallas import tpu as pltpu
from jax.sharding import PartitionSpec as P

HD = 128
CHUNK = 128
TILE = 256
NEG = -1e30
SAFE = 60.0
LAST = (((1,), (1,)), ((), ()))


PIECES = 4


def attention_kernel(total, start_ref, lengths_ref, row_ref, q_hbm, do_hbm, kv_hbm,
                     dq_hbm, dkv_hbm, q_ref, do_ref, kv_ref, dq_ref, dkv_ref, load_sem, store_sem, e_ref, ds_ref, mt_ref, q_rows, do_rows, q_over, do_over, kt_ref, dqt_ref,
                     dk_acc, dv_acc, stat_ref):
    rows = q_rows.shape[0]
    heads = rows // CHUNK
    pair = 2 * CHUNK
    pairs = rows // pair
    chunks = q_ref.shape[0] // CHUNK
    tiles = total // TILE
    scale = HD ** -0.5
    to_log2 = scale * 1.4426950408889634

    piece = total // PIECES
    loads = [pltpu.make_async_copy(kv_hbm.at[pl.ds(n * piece, piece), :], kv_ref.at[pl.ds(n * piece, piece), :],
                                   load_sem.at[n]) for n in range(PIECES)]
    loads += [pltpu.make_async_copy(q_hbm, q_ref, load_sem.at[PIECES]),
              pltpu.make_async_copy(do_hbm, do_ref, load_sem.at[PIECES + 1])]
    for copy in loads:
        copy.start()

    def clear(i, _):
        at = pl.ds(pl.multiple_of(i * TILE, TILE), TILE)
        dk_acc[at, :] = jnp.zeros((TILE, HD), jnp.float32)
        dv_acc[at, :] = jnp.zeros((TILE, HD), jnp.float32)
        return 0

    lax.fori_loop(0, tiles, clear, 0)

    def turn_keys(i, most):
        turned = kv_ref[pl.ds(pl.multiple_of(i * TILE, TILE), TILE), :HD].T
        kt_ref[i] = turned
        wide = turned.astype(jnp.float32)
        return jnp.maximum(most, jnp.sum(wide * wide, axis=0, keepdims=True))

    key_most = jnp.zeros((1, TILE), jnp.float32)
    for n in range(PIECES):
        loads[n].wait()
        key_most = lax.fori_loop(n * tiles // PIECES, (n + 1) * tiles // PIECES, turn_keys, key_most, unroll=4)
    key_most = jnp.max(key_most)
    for copy in loads[PIECES:]:
        copy.wait()

    def one_chunk(j, _):
        first = start_ref[j]
        t0 = pl.multiple_of(j * CHUNK, CHUNK)
        for h in range(heads):
            part = q_ref[pl.ds(t0, CHUNK), h * HD:(h + 1) * HD]
            q_rows[h * CHUNK:(h + 1) * CHUNK, :] = part
            do_rows[h * CHUNK:(h + 1) * CHUNK, :] = do_ref[pl.ds(t0, CHUNK), h * HD:(h + 1) * HD]
        small = jnp.max(row_ref[heads:, pl.ds(t0, CHUNK)]) * key_most * (to_log2 * to_log2) <= SAFE * SAFE
        query_pos = first + lax.broadcasted_iota(jnp.int32, (1, pair), 1) % CHUNK
        row_start = jnp.zeros((1, pair), jnp.int32)
        low, high = jnp.int32(0), jnp.int32(0)
        begin = jnp.int32(0)
        for d in range(lengths_ref.shape[0]):
            row_start = jnp.where(query_pos >= begin, begin, row_start)
            low = jnp.where(first >= begin, begin, low)
            high = jnp.where(first + CHUNK - 1 >= begin, begin, high)
            begin = begin + lengths_ref[d]
        tile_low = low // TILE
        tile_end = (first + CHUNK - 1) // TILE + 1
        plain_low = jnp.minimum((high + TILE - 1) // TILE, tile_end)
        plain_end = jnp.maximum((first + 1) // TILE, plain_low)
        edge = plain_low - tile_low
        edges = edge + tile_end - plain_end

        def edge_tile(n):
            return jnp.where(n < edge, tile_low + n, plain_end + n - edge)

        def allowed_of(key0):
            key_pos = key0 + lax.broadcasted_iota(jnp.int32, (TILE, pair), 0)
            return (key_pos >= row_start) & (key_pos <= query_pos)

        def scores(key, p):
            return lax.dot_general(key, q_rows[p * pair:(p + 1) * pair, :], LAST,
                                   preferred_element_type=jnp.float32) * to_log2

        def weigh(i, sums, masked):
            key0 = pl.multiple_of(i * TILE, TILE)
            key = kv_ref[pl.ds(key0, TILE), :HD]
            new = []
            for p in range(pairs):
                e = jnp.exp2(scores(key, p))
                if masked:
                    e = jnp.where(allowed_of(key0), e, 0.0)
                new.append(sums[p] + jnp.sum(e.reshape(TILE // 8, 8, pair), axis=0))
                e_ref[i - tile_low, :, p * pair:(p + 1) * pair] = e.astype(jnp.bfloat16)
            return tuple(new)

        @pl.when(small)
        def _():
            sums = tuple(jnp.zeros((8, pair), jnp.float32) for _ in range(pairs))
            sums = lax.fori_loop(0, edges, lambda n, s: weigh(edge_tile(n), s, True), sums)
            sums = lax.fori_loop(plain_low, plain_end, lambda i, s: weigh(i, s, False), sums)
            for p in range(pairs):
                stat_ref[:, p * pair:(p + 1) * pair] = 1.0 / jnp.sum(sums[p], axis=0, keepdims=True)

        @pl.when(jnp.logical_not(small))
        def _():
            def step(i, carry):
                tops, sums = carry
                key0 = pl.multiple_of(i * TILE, TILE)
                key = kv_ref[pl.ds(key0, TILE), :HD]
                new_tops, new_sums = [], []
                for p in range(pairs):
                    s = jnp.where(allowed_of(key0), scores(key, p), NEG)
                    top = jnp.maximum(tops[p], jnp.max(s, axis=0, keepdims=True))
                    e = jnp.exp2(s - top)
                    new_sums.append(sums[p] * jnp.exp2(tops[p] - top) + jnp.sum(e, axis=0, keepdims=True))
                    new_tops.append(top)
                    e_ref[i - tile_low, :, p * pair:(p + 1) * pair] = e.astype(jnp.bfloat16)
                    mt_ref[i - tile_low, :, p * pair:(p + 1) * pair] = top
                return tuple(new_tops), tuple(new_sums)

            tops, sums = lax.fori_loop(tile_low, tile_end, step, (
                tuple(jnp.full((1, pair), NEG, jnp.float32) for _ in range(pairs)),
                tuple(jnp.zeros((1, pair), jnp.float32) for _ in range(pairs))))

            def settle(i, _):
                for p in range(pairs):
                    part = slice(p * pair, (p + 1) * pair)
                    factor = jnp.exp2(mt_ref[i - tile_low, :, part] - tops[p])
                    e_ref[i - tile_low, :, part] = (
                        e_ref[i - tile_low, :, part].astype(jnp.float32) * factor).astype(jnp.bfloat16)
                return 0

            lax.fori_loop(tile_low, tile_end, settle, 0)
            for p in range(pairs):
                stat_ref[:, p * pair:(p + 1) * pair] = 1.0 / sums[p]

        for h in range(heads):
            part = slice(h * CHUNK, (h + 1) * CHUNK)
            inverse = jnp.broadcast_to(stat_ref[:, part], (HD, CHUNK)).T
            q_over[part, :] = (q_rows[part, :].astype(jnp.float32) * inverse).astype(jnp.bfloat16)
            do_over[part, :] = (do_rows[part, :].astype(jnp.float32) * inverse).astype(jnp.bfloat16)
        delta = [jnp.concatenate([row_ref[2 * p:2 * p + 1, pl.ds(t0, CHUNK)],
                                  row_ref[2 * p + 1:2 * p + 2, pl.ds(t0, CHUNK)]], axis=1) for p in range(pairs)]
        dqt_ref[...] = jnp.zeros_like(dqt_ref)

        def grad_step(i, _):
            key0 = pl.multiple_of(i * TILE, TILE)
            slot = i - tile_low
            value = kv_ref[pl.ds(key0, TILE), HD:]
            key_t = kt_ref[i]
            for p in range(pairs):
                part = slice(p * pair, (p + 1) * pair)
                dp = lax.dot_general(value, do_rows[part, :], LAST, preferred_element_type=jnp.float32)
                ds_ref[:, part] = (e_ref[slot, :, part].astype(jnp.float32) * (dp - delta[p])).astype(jnp.bfloat16)
            dv_acc[pl.ds(key0, TILE), :] += jnp.dot(e_ref[slot], do_over[...], preferred_element_type=jnp.float32)
            dk_acc[pl.ds(key0, TILE), :] += jnp.dot(ds_ref[...], q_over[...], preferred_element_type=jnp.float32)
            dqt_ref[...] += jnp.dot(key_t, ds_ref[...], preferred_element_type=jnp.float32)
            return 0

        lax.fori_loop(tile_low, tile_end, grad_step, 0)
        for h in range(heads):
            part = slice(h * CHUNK, (h + 1) * CHUNK)
            dq_ref[pl.ds(t0, CHUNK), h * HD:(h + 1) * HD] = (
                dqt_ref[:, part] * (stat_ref[:, part] * scale)).T.astype(jnp.bfloat16)
        pltpu.make_async_copy(dq_ref.at[pl.ds(t0, CHUNK), :], dq_hbm.at[pl.ds(t0, CHUNK), :], store_sem.at[j]).start()
        return 0

    lax.fori_loop(0, chunks, one_chunk, 0)

    def write(i, _):
        at = pl.ds(pl.multiple_of(i * TILE, TILE), TILE)
        dkv_ref[at, :HD] = (dk_acc[at, :] * scale).astype(jnp.bfloat16)
        dkv_ref[at, HD:] = dv_acc[at, :].astype(jnp.bfloat16)
        return 0

    stores = []
    for n in range(PIECES):
        lax.fori_loop(n * tiles // PIECES, (n + 1) * tiles // PIECES, write, 0)
        stores.append(pltpu.make_async_copy(dkv_ref.at[pl.ds(n * piece, piece), :],
                                            dkv_hbm.at[pl.ds(n * piece, piece), :], store_sem.at[chunks + n]))
        stores[-1].start()
    for j in range(chunks):
        part = pl.ds(j * CHUNK, CHUNK)
        pltpu.make_async_copy(dq_ref.at[part, :], dq_hbm.at[part, :], store_sem.at[j]).wait()
    for copy in stores:
        copy.wait()


def attention(starts, lengths, q, do, row_info, kv, longest=4608):
    total = kv.shape[0]
    rows = q.shape[1] // HD * CHUNK
    max_tiles = (longest + CHUNK) // TILE + 2
    vmem = pl.BlockSpec(memory_space=pltpu.VMEM)
    smem = pl.BlockSpec(memory_space=pltpu.SMEM)
    anywhere = pl.BlockSpec(memory_space=pl.ANY)
    return pl.pallas_call(
        functools.partial(attention_kernel, total),
        out_shape=[jax.ShapeDtypeStruct(q.shape, jnp.bfloat16),
                   jax.ShapeDtypeStruct(kv.shape, jnp.bfloat16)],
        in_specs=[smem, smem, vmem] + [anywhere] * 3,
        out_specs=[anywhere] * 2,
        scratch_shapes=[
            pltpu.VMEM(q.shape, jnp.bfloat16),
            pltpu.VMEM(q.shape, jnp.bfloat16),
            pltpu.VMEM(kv.shape, jnp.bfloat16),
            pltpu.VMEM(q.shape, jnp.bfloat16),
            pltpu.VMEM(kv.shape, jnp.bfloat16),
            pltpu.SemaphoreType.DMA((PIECES + 2,)),
            pltpu.SemaphoreType.DMA((q.shape[0] // CHUNK + PIECES,)),
            pltpu.VMEM((max_tiles, TILE, rows), jnp.bfloat16),
            pltpu.VMEM((TILE, rows), jnp.bfloat16),
            pltpu.VMEM((max_tiles, 1, rows), jnp.float32),
            pltpu.VMEM((rows, HD), jnp.bfloat16),
            pltpu.VMEM((rows, HD), jnp.bfloat16),
            pltpu.VMEM((rows, HD), jnp.bfloat16),
            pltpu.VMEM((rows, HD), jnp.bfloat16),
            pltpu.VMEM((total // TILE, HD, TILE), jnp.bfloat16),
            pltpu.VMEM((HD, rows), jnp.float32),
            pltpu.VMEM((total, HD), jnp.float32),
            pltpu.VMEM((total, HD), jnp.float32),
            pltpu.VMEM((1, rows), jnp.float32),
        ],
        compiler_params=pltpu.CompilerParams(vmem_limit_bytes=62 * 2**20),
        name="attention",
    )(starts, lengths, row_info, q, do, kv)


SIDE = 4
MESH = pl.DeviceIdType.MESH


def ring_place(axis, step):
    me = lax.axis_index("ctx")
    x, z = me // SIDE, me % SIDE
    if axis == 0:
        return lax.rem(x + step + 2 * SIDE, SIDE) * SIDE + z
    return x * SIDE + lax.rem(z + step + SIDE, SIDE)


def block_at(axis, first, second):
    me = lax.axis_index("ctx")
    x, z = me // SIDE, me % SIDE
    along, across = (first, second) if axis == 0 else (second, first)
    return lax.rem(x + along + SIDE, SIDE) * SIDE + lax.rem(z + across + SIDE, SIDE)


def greet(partners):
    barrier = pltpu.get_barrier_semaphore()
    for partner in partners:
        pl.semaphore_signal(barrier, inc=1, device_id=partner, device_id_type=MESH)
    pl.semaphore_wait(barrier, len(partners))


RELAY = ((1, 0), (-1, 1))


def collect_kernel(k_ref, v_ref, q_ref, out_grad_ref, outputs_ref, kv_hbm, q_out, out_grad_out, row_out,
                   kv_ref, k_vmem, v_vmem, q_vmem, out_grad_vmem, outputs_vmem, row_vmem, relay, local_sem, out_sem, send_sem, recv_sem):
    me = lax.axis_index("ctx")
    rows = k_ref.shape[0]
    half = rows // 2
    mid = half // 2
    quarter = rows // SIDE
    own = [
        pltpu.make_async_copy(k_ref, k_vmem, local_sem.at[0]),
        pltpu.make_async_copy(v_ref, v_vmem, local_sem.at[1]),
    ]
    kept = [
        pltpu.make_async_copy(q_ref, q_vmem, local_sem.at[2]),
        pltpu.make_async_copy(out_grad_ref, out_grad_vmem, local_sem.at[3]),
        pltpu.make_async_copy(outputs_ref, outputs_vmem, local_sem.at[4]),
    ]
    for copy in own + kept:
        copy.start()
    for copy in own:
        copy.wait()
    kv_ref[me, :, :HD] = k_vmem[...]
    kv_ref[me, :, HD:] = v_vmem[...]
    greet([{"ctx": ring_place(axis, step)} for axis, step in ((0, 1), (0, -1), (0, 2), (1, 1), (1, -1))])
    copies = {}

    def begin(name, number, place, src, dst):
        copy = pltpu.make_async_remote_copy(
            src_ref=src, dst_ref=dst, send_sem=send_sem.at[number], recv_sem=recv_sem.at[number],
            device_id={"ctx": ring_place(*place)}, device_id_type=MESH)
        copy.start()
        copies[name] = copy

    def pass_on(name, number, place, block, start, count):
        region = kv_ref.at[block, pl.ds(start, count), :]
        begin(name, number, place, region, region)

    def near(h, item, shift):
        axis = 0 if item == "line" else 1
        base = h * 20 + (0 if item == "line" else 4 + 4 * item)
        block = me if item == "line" else block_at(0, shift, 0)
        pass_on((h, item, 0), base, (axis, 1), block, h * half, half)
        pass_on((h, item, 1), base + 1, (axis, -1), block, h * half, half)

    def far(h, item, shift):
        axis = 0 if item == "line" else 1
        base = h * 20 + (0 if item == "line" else 4 + 4 * item)

        def block(step):
            return block_at(0, step, 0) if item == "line" else block_at(0, shift, step)

        copies[h, item, 0].wait_recv()
        pass_on((h, item, 2), base + 2, (axis, 1), block(-1), h * half, mid)
        copies[h, item, 1].wait_recv()
        pass_on((h, item, 3), base + 3, (axis, -1), block(1), h * half + mid, mid)

    stores = []

    def keep(block, h):
        region = pl.ds(h * half, half)
        stores.append(pltpu.make_async_copy(kv_ref.at[block, region, :], kv_hbm.at[block, region, :],
                                            out_sem.at[len(stores)]))
        stores[-1].start()

    shifts = (0, -1, 1, 2)
    pairs = ((q_ref, q_out), (out_grad_ref, out_grad_out))
    for h in (0, 1):
        near(h, "line", 0)
    for h in (0, 1):
        near(h, 0, shifts[0])
    for h in (0, 1):
        far(h, "line", 0)
        near(h, 1, shifts[1])
        near(h, 2, shifts[2])
    for n, (src, dst) in enumerate(pairs):
        for step, slot in RELAY:
            part = pl.ds(2 * quarter + slot * (quarter // 2), quarter // 2)
            begin(("relay", n, slot), 40 + 2 * n + slot, (0, step), src.at[part, :], relay.at[n, slot])
    for n, (src, dst) in enumerate(pairs):
        for j, step in ((1, 1), (3, -1)):
            part = pl.ds(j * quarter, quarter)
            begin(("move", n, j), 44 + 2 * n + j // 2, (0, step), src.at[part, :], dst.at[part, :])
    for copy in kept:
        copy.wait()
    stay = [
        pltpu.make_async_copy(q_vmem.at[pl.ds(0, quarter), :], q_out.at[pl.ds(0, quarter), :], local_sem.at[0]),
        pltpu.make_async_copy(out_grad_vmem.at[pl.ds(0, quarter), :], out_grad_out.at[pl.ds(0, quarter), :],
                              local_sem.at[1]),
    ]
    for copy in stay:
        copy.start()
    for h in (0, 1):
        for shift in (0, -1, 1):
            keep(block_at(0, shift, 0), h)
    heads = row_vmem.shape[0] // 2
    for head in range(heads):
        part = slice(head * HD, (head + 1) * HD)
        grad = out_grad_vmem[:, part].astype(jnp.float32)
        query = q_vmem[:, part].astype(jnp.float32)
        row_vmem[head:head + 1, :] = jnp.sum((grad * outputs_vmem[:, part].astype(jnp.float32)).T, axis=0, keepdims=True)
        row_vmem[heads + head:heads + head + 1, :] = jnp.sum((query * query).T, axis=0, keepdims=True)
    for j, step in ((1, 1), (2, 2), (3, -1)):
        part = pl.ds(j * quarter, quarter)
        begin(("rows", j), 51 + j, (0, step), row_vmem.at[:, part], row_out.at[:, part])
    row_out[:, :quarter] = row_vmem[:, :quarter]
    for h in (0, 1):
        far(h, 0, shifts[0])
        keep(block_at(0, 0, 1), h)
        keep(block_at(0, 0, -1), h)
    for h in (0, 1):
        copies[h, "line", 2].wait_recv()
        copies[h, "line", 3].wait_recv()
        near(h, 3, shifts[3])
        keep(block_at(0, 2, 0), h)
    for n, (src, dst) in enumerate(pairs):
        for step, slot in RELAY:
            part = pl.ds(2 * quarter + slot * (quarter // 2), quarter // 2)
            copies["relay", n, slot].wait_recv()
            begin(("relayed", n, slot), 48 + 2 * n + slot, (0, step), relay.at[n, slot], dst.at[part, :])
    for item in (1, 2, 3):
        for h in (0, 1):
            far(h, item, shifts[item])
            keep(block_at(0, shifts[item], 1), h)
            keep(block_at(0, shifts[item], -1), h)
    for item in (0, 1, 2, 3):
        for h in (0, 1):
            copies[h, item, 2].wait_recv()
            copies[h, item, 3].wait_recv()
            keep(block_at(0, shifts[item], 2), h)
    for n in (0, 1):
        for name in (("move", n, 1), ("move", n, 3), ("relayed", n, 0), ("relayed", n, 1)):
            copies[name].wait_recv()
    for j in (1, 2, 3):
        copies["rows", j].wait_recv()
    for copy in stay + stores:
        copy.wait()
    for copy in copies.values():
        copy.wait_send()


def collect(keys, values, queries, out_grad, outputs):
    rows = keys.shape[0]
    heads = out_grad.shape[1] // HD
    bf = jnp.bfloat16
    vmem = pl.BlockSpec(memory_space=pltpu.VMEM)
    anywhere = pl.BlockSpec(memory_space=pl.ANY)
    return pl.pallas_call(
        collect_kernel,
        out_shape=[jax.ShapeDtypeStruct((SIDE * SIDE, rows, 2 * HD), bf),
                   jax.ShapeDtypeStruct(queries.shape, bf),
                   jax.ShapeDtypeStruct(queries.shape, bf),
                   jax.ShapeDtypeStruct((2 * heads, rows), jnp.float32)],
        in_specs=[anywhere] * 5,
        out_specs=[anywhere] * 3 + [vmem],
        scratch_shapes=[pltpu.VMEM((SIDE * SIDE, rows, 2 * HD), bf), pltpu.VMEM(keys.shape, bf), pltpu.VMEM(keys.shape, bf), pltpu.VMEM(queries.shape, bf), pltpu.VMEM(queries.shape, bf), pltpu.VMEM(queries.shape, bf),
                        pltpu.VMEM((2 * heads, rows), jnp.float32),
                        pltpu.VMEM((2, 2, rows // SIDE // 2, queries.shape[1]), bf),
                        pltpu.SemaphoreType.DMA((5,)), pltpu.SemaphoreType.DMA((2 * SIDE * SIDE,)), pltpu.SemaphoreType.DMA((55,)), pltpu.SemaphoreType.DMA((55,))],
        compiler_params=pltpu.CompilerParams(collective_id=0, has_side_effects=True, vmem_limit_bytes=62 * 2**20),
        name="collect",
    )(keys, values, queries, out_grad, outputs)


PARTS = 4
PART_ORDER = (0, 1, 3, 2)
FIRST_AXIS = ((0, 0), (0, 0), (0, 1), (0, 1))
RS_ORDER = (2, -1, 1, 0)


def tp_place(step, core):
    y = lax.axis_index("tp") // 2
    return lax.rem(y + step + SIDE, SIDE) * 2 + core


def finish_kernel(dq_in, dkv_hbm, wq_hbm, wk_hbm, wv_hbm, out_ref, dkv_ref, dq_ref, relay, wq_ref, wk_ref, wv_ref, wkv_ref, acc_ref, sum_ref,
                  low_ref, high_ref, stage_ref, fin_ref, res_ref, pair_out, pair_in, y_stage, y_low, y_high, y_fin,
                  load_sem, send_sem, recv_sem):
    core = lax.axis_index("tp") % 2
    rows = dq_ref.shape[0]
    part_rows = rows // PARTS
    size = part_rows // 2
    mid = size // 2
    loads = [
        pltpu.make_async_copy(dkv_hbm, dkv_ref, load_sem.at[0]),
        pltpu.make_async_copy(wq_hbm, wq_ref, load_sem.at[1]),
        pltpu.make_async_copy(wk_hbm, wk_ref, load_sem.at[2]),
        pltpu.make_async_copy(wv_hbm, wv_ref, load_sem.at[3]),
        pltpu.make_async_copy(dq_in.at[pl.ds(0, part_rows), :], dq_ref.at[pl.ds(0, part_rows), :], load_sem.at[4]),
    ]
    for copy in loads:
        copy.start()
    greet([{"ctx": ring_place(axis, step)} for axis in (0, 1) for step in (1, -1)]
          + [{"tp": tp_place(step, core)} for step in (1, -1)] + [{"tp": tp_place(0, 1 - core)}])
    copies = {}

    def begin(name, number, device, src, dst):
        copy = pltpu.make_async_remote_copy(src_ref=src, dst_ref=dst, send_sem=send_sem.at[number],
                                            recv_sem=recv_sem.at[number], device_id=device, device_id_type=MESH)
        copy.start()
        copies[name] = copy

    def wide(value):
        return value.astype(jnp.float32)

    def rows_of(s, h):
        return pl.ds(s * part_rows + h * size, size)

    def ident(s, h, k):
        return (s * 2 + h) * 5 + (4 if k is None else RS_ORDER.index(k))

    def term(s, h, k, shift, start, count):
        if k is None:
            return res_ref.at[s, h, RS_ORDER.index(shift), pl.ds(start, count), :]
        return dkv_ref.at[block_at(FIRST_AXIS[s][h], k, shift), pl.ds(s * part_rows + h * size + start, count), :]

    def ring_axis(s, h, k):
        return FIRST_AXIS[s][h] if k is None else 1 - FIRST_AXIS[s][h]

    def reduce_send(s, h, k):
        n, axis = ident(s, h, k), ring_axis(s, h, k)
        begin(("low", n), 4 * n, {"ctx": ring_place(axis, 1)}, term(s, h, k, 2, 0, mid), low_ref.at[n])
        begin(("high", n), 4 * n + 1, {"ctx": ring_place(axis, -1)}, term(s, h, k, 2, mid, mid), high_ref.at[n])

    def reduce_pass(s, h, k):
        n, axis = ident(s, h, k), ring_axis(s, h, k)
        copies["low", n].wait_recv()
        stage_ref[n, 0, :mid, :] = (wide(term(s, h, k, 1, 0, mid)[...]) + wide(low_ref[n])).astype(jnp.bfloat16)
        stage_ref[n, 0, mid:, :] = term(s, h, k, 1, mid, mid)[...]
        begin(("up", n), 4 * n + 2, {"ctx": ring_place(axis, 1)}, stage_ref.at[n, 0], fin_ref.at[n, 0])
        copies["high", n].wait_recv()
        stage_ref[n, 1, :mid, :] = term(s, h, k, -1, 0, mid)[...]
        stage_ref[n, 1, mid:, :] = (wide(term(s, h, k, -1, mid, mid)[...]) + wide(high_ref[n])).astype(jnp.bfloat16)
        begin(("down", n), 4 * n + 3, {"ctx": ring_place(axis, -1)}, stage_ref.at[n, 1], fin_ref.at[n, 1])

    def reduce_end(s, h, k):
        n = ident(s, h, k)
        copies["up", n].wait_recv()
        copies["down", n].wait_recv()
        total = wide(term(s, h, k, 0, 0, size)[...]) + wide(fin_ref[n, 0]) + wide(fin_ref[n, 1])
        if k is None:
            sum_ref[rows_of(s, h), :] = total.astype(jnp.bfloat16)
        else:
            res_ref[s, h, RS_ORDER.index(k)] = total.astype(jnp.bfloat16)

    def reduce_steps(s):
        for k in RS_ORDER:
            for h in (0, 1):
                reduce_send(s, h, k)
        yield
        for k in RS_ORDER:
            for h in (0, 1):
                reduce_pass(s, h, k)
        yield
        for h in (0, 1):
            reduce_end(s, h, 2)
            reduce_send(s, h, None)
        yield
        for h in (0, 1):
            reduce_end(s, h, -1)
            reduce_end(s, h, 1)
        for h in (0, 1):
            reduce_pass(s, h, None)
        yield
        for h in (0, 1):
            reduce_end(s, h, 0)
        yield
        for h in (0, 1):
            reduce_end(s, h, None)
        yield

    def project(g, n):
        part = pl.ds(n * (rows // 2), rows // 2)
        acc_ref[g, part, :] = lax.dot_general(dq_ref[part, :], wq_ref[g], LAST, preferred_element_type=jnp.float32)

    back = 48 * PARTS

    def give_back():
        for step, slot in RELAY:
            part = pl.ds(2 * part_rows + slot * size, size)
            begin(("relay", slot), back + slot, {"ctx": ring_place(0, step)}, dq_in.at[part, :], relay.at[slot])
        for j, step in ((1, -1), (3, 1)):
            part = pl.ds(j * part_rows, part_rows)
            begin(("back", j), back + 2 + j // 2, {"ctx": ring_place(0, step)}, dq_in.at[part, :], dq_ref.at[part, :])

    def relay_back():
        for step, slot in RELAY:
            part = pl.ds(2 * part_rows + slot * size, size)
            copies["relay", slot].wait_recv()
            begin(("relayed", slot), back + 4 + slot, {"ctx": ring_place(0, step)}, relay.at[slot], dq_ref.at[part, :])

    far = 40 * PARTS

    def spread(s, step):
        n = s * 4 + RS_ORDER.index(step)
        other, mine = tp_place(step, 1 - core), tp_place(step, core)
        part = pl.ds(s * part_rows, part_rows)
        low = sum_ref[part, :]
        total = acc_ref[other, part, :] + lax.dot_general(low, wkv_ref[other], LAST, preferred_element_type=jnp.float32)
        pair_out[n, 0] = total[:size].astype(jnp.bfloat16)
        pair_out[n, 1] = total[size:].astype(jnp.bfloat16)
        begin(("pair", n), far + n, {"tp": tp_place(0, 1 - core)}, pair_out.at[n], pair_in.at[n])
        acc_ref[mine, part, :] += lax.dot_general(low, wkv_ref[mine], LAST, preferred_element_type=jnp.float32)

    def chip_sum(s, step, h):
        n = s * 4 + RS_ORDER.index(step)
        return acc_ref[tp_place(step, core), rows_of(s, h), :] + wide(pair_in[n, h])

    def y_send(s):
        copies["pair", s * 4].wait_recv()
        for h in (0, 1):
            y_stage[s, 0, h] = chip_sum(s, 2, h).astype(jnp.bfloat16)
        number = far + 4 * PARTS + 4 * s
        begin(("y_low", s), number, {"tp": tp_place(1, core)}, y_stage.at[s, 0, 0], y_low.at[s])
        begin(("y_high", s), number + 1, {"tp": tp_place(-1, core)}, y_stage.at[s, 0, 1], y_high.at[s])

    def y_pass(s, step):
        number = far + 4 * PARTS + 4 * s
        copies["pair", s * 4 + RS_ORDER.index(step)].wait_recv()
        slot, low = (1, 0) if step == 1 else (2, 1)
        y_stage[s, slot, 1 - low] = chip_sum(s, step, 1 - low).astype(jnp.bfloat16)
        copies["y_low" if step == 1 else "y_high", s].wait_recv()
        came = y_low if step == 1 else y_high
        y_stage[s, slot, low] = (chip_sum(s, step, low) + wide(came[s])).astype(jnp.bfloat16)
        begin(("y_fin", s, step), number + 1 + slot, {"tp": tp_place(step, core)}, y_stage.at[s, slot],
              y_fin.at[s, slot - 1])

    def y_end(s):
        copies["pair", s * 4 + 3].wait_recv()
        copies["y_fin", s, 1].wait_recv()
        copies["y_fin", s, -1].wait_recv()
        for h in (0, 1):
            out_ref[rows_of(s, h), :] = (
                chip_sum(s, 0, h) + wide(y_fin[s, 0, h]) + wide(y_fin[s, 1, h])).astype(jnp.bfloat16)

    sums = {s: reduce_steps(s) for s in PART_ORDER}
    one, two, three, four = PART_ORDER
    loads[0].wait()
    next(sums[one])
    next(sums[two])
    give_back()
    next(sums[one])
    next(sums[three])
    next(sums[two])
    next(sums[one])
    relay_back()
    next(sums[one])
    loads[1].wait()
    loads[4].wait()
    copies["back", 1].wait_recv()
    for g in range(0, 4):
        project(g, 0)
    next(sums[one])
    next(sums[two])
    next(sums[three])
    next(sums[four])
    for g in range(4, 8):
        project(g, 0)
    loads[2].wait()
    loads[3].wait()

    def merge(g, _):
        wkv_ref[g, :, :HD] = wk_ref[g]
        wkv_ref[g, :, HD:] = wv_ref[g]
        return 0

    lax.fori_loop(0, wkv_ref.shape[0], merge, 0)
    next(sums[one])
    next(sums[two])
    for step in (2, 1):
        spread(one, step)
    next(sums[two])
    next(sums[three])
    next(sums[four])
    y_send(one)
    for step in (-1, 0):
        spread(one, step)
    copies["back", 3].wait_recv()
    copies["relayed", 0].wait_recv()
    copies["relayed", 1].wait_recv()
    for g in range(0, 4):
        project(g, 1)
    next(sums[two])
    next(sums[three])
    y_pass(one, 1)
    y_pass(one, -1)
    for step in RS_ORDER:
        spread(two, step)
    next(sums[four])
    next(sums[three])
    y_send(two)
    for g in range(4, 8):
        project(g, 1)
    next(sums[three])
    next(sums[four])
    y_pass(two, 1)
    y_pass(two, -1)
    for step in RS_ORDER:
        spread(three, step)
    next(sums[four])
    y_send(three)
    next(sums[four])
    for step in RS_ORDER:
        spread(four, step)
    y_end(one)
    y_pass(three, 1)
    y_pass(three, -1)
    y_send(four)
    y_end(two)
    y_pass(four, 1)
    y_pass(four, -1)
    y_end(three)
    y_end(four)
    for copy in copies.values():
        copy.wait_send()


def finish(query_grad, terms, w_query, w_key, w_value):
    rows = query_grad.shape[0]
    blocks = SIDE * 2
    columns = w_query.shape[0] // blocks
    size = rows // PARTS // 2
    mid = size // 2
    reduces = 10 * PARTS
    sems = 4 * reduces + 8 * PARTS + 6
    bf = jnp.bfloat16
    vmem = pl.BlockSpec(memory_space=pltpu.VMEM)
    anywhere = pl.BlockSpec(memory_space=pl.ANY)
    return pl.pallas_call(
        finish_kernel,
        out_shape=jax.ShapeDtypeStruct((rows, columns), bf),
        in_specs=[anywhere] * 5,
        out_specs=vmem,
        scratch_shapes=[
            pltpu.VMEM(terms.shape, bf),
            pltpu.VMEM(query_grad.shape, bf),
            pltpu.VMEM((2, size, query_grad.shape[1]), bf),
            pltpu.VMEM((blocks, columns, w_query.shape[1]), bf),
            pltpu.VMEM((blocks, columns, HD), bf),
            pltpu.VMEM((blocks, columns, HD), bf),
            pltpu.VMEM((blocks, columns, 2 * HD), bf),
            pltpu.VMEM((blocks, rows, columns), jnp.float32),
            pltpu.VMEM((rows, 2 * HD), bf),
            pltpu.VMEM((reduces, mid, 2 * HD), bf),
            pltpu.VMEM((reduces, mid, 2 * HD), bf),
            pltpu.VMEM((reduces, 2, size, 2 * HD), bf),
            pltpu.VMEM((reduces, 2, size, 2 * HD), bf),
            pltpu.VMEM((PARTS, 2, 4, size, 2 * HD), bf),
            pltpu.VMEM((4 * PARTS, 2, size, columns), bf),
            pltpu.VMEM((4 * PARTS, 2, size, columns), bf),
            pltpu.VMEM((PARTS, 3, 2, size, columns), bf),
            pltpu.VMEM((PARTS, size, columns), bf),
            pltpu.VMEM((PARTS, size, columns), bf),
            pltpu.VMEM((PARTS, 2, 2, size, columns), bf),
            pltpu.SemaphoreType.DMA((5,)),
            pltpu.SemaphoreType.DMA((sems,)),
            pltpu.SemaphoreType.DMA((sems,)),
        ],
        compiler_params=pltpu.CompilerParams(collective_id=1, has_side_effects=True, vmem_limit_bytes=62 * 2**20),
        name="finish",
    )(query_grad, terms, w_query.reshape(blocks, columns, -1), w_key.reshape(blocks, columns, -1),
      w_value.reshape(blocks, columns, -1))


def shards(queries, keys, values, outputs, out_grad, lengths, w_query, w_key, w_value):
    rows = queries.shape[0]
    starts = jnp.stack([ring_place(0, -j) * rows + j * CHUNK for j in range(SIDE)]).astype(jnp.int32)
    collected, q_work, grad_work, row_info = collect(keys, values, queries, out_grad, outputs)
    query_grad, terms = attention(starts, lengths, q_work, grad_work, row_info, collected.reshape(-1, 2 * HD))
    return finish(query_grad, terms.reshape(collected.shape), w_query, w_key, w_value)


def solution(mesh):
    in_specs = (P("ctx", "tp"),) * 5 + (P(),) + (P(None, "tp"),) * 3
    return jax.shard_map(shards, mesh=mesh, in_specs=in_specs, out_specs=P("ctx", "tp"), check_vma=False)
```

```python
import functools
import jax, jax.numpy as jnp
from jax import lax
from jax.experimental import pallas as pl
from jax.experimental.pallas import tpu as pltpu
from jax.sharding import PartitionSpec as P

HD = 128
CHUNK = 128
TILE = 256
NEG = -1e30
SAFE = 60.0
LAST = (((1,), (1,)), ((), ()))
PIECES = 4


def attention_kernel(total, start_ref, lengths_ref, row_ref, q_hbm, do_hbm, kv_hbm, dq_hbm, dkv_hbm,
                     q_ref, do_ref, kv_ref, dq_ref, dkv_ref, load_sem, store_sem, e_ref, ds_ref, ds_other, q_rows, do_rows,
                     q_turned, do_turned, delta_ref, top_ref, sum_ref, dq_acc, dk_acc, dv_acc):
    rows = q_rows.shape[0]
    heads = rows // CHUNK
    pair = 2 * CHUNK
    pairs = rows // pair
    chunks = q_ref.shape[0] // CHUNK
    blocks = total // HD
    scale = HD ** -0.5
    to_log2 = scale * 1.4426950408889634
    piece = total // PIECES
    loads = [pltpu.make_async_copy(kv_hbm.at[pl.ds(n * piece, piece), :],
                                   kv_ref.at[pl.ds(CHUNK + n * piece, piece), :], load_sem.at[n])
             for n in range(PIECES)]
    loads += [pltpu.make_async_copy(q_hbm, q_ref, load_sem.at[PIECES]),
              pltpu.make_async_copy(do_hbm, do_ref, load_sem.at[PIECES + 1])]
    for copy in loads:
        copy.start()
    kv_ref[:CHUNK, :] = jnp.zeros((CHUNK, 2 * HD), jnp.bfloat16)

    def clear(i, _):
        dk_acc[i] = jnp.zeros((HD, HD), jnp.float32)
        dv_acc[i] = jnp.zeros((HD, HD), jnp.float32)
        return 0

    lax.fori_loop(0, blocks + 1, clear, 0)

    def measure_keys(i, most):
        wide = kv_ref[pl.ds(pl.multiple_of(CHUNK + i * TILE, CHUNK), TILE), :HD].astype(jnp.float32)
        return jnp.maximum(most, jnp.sum(wide * wide, axis=1, keepdims=True))

    key_most = jnp.zeros((TILE, 1), jnp.float32)
    for n in range(PIECES):
        loads[n].wait()
        key_most = lax.fori_loop(n * piece // TILE, (n + 1) * piece // TILE, measure_keys, key_most)
    key_most = jnp.max(key_most)
    for copy in loads[PIECES:]:
        copy.wait()

    def one_chunk(j, _):
        first = start_ref[j]
        end = first + CHUNK
        t0 = pl.multiple_of(j * CHUNK, CHUNK)
        for h in range(heads):
            part = slice(h * CHUNK, (h + 1) * CHUNK)
            q_rows[part, :] = q_ref[pl.ds(t0, CHUNK), h * HD:(h + 1) * HD]
            do_rows[part, :] = do_ref[pl.ds(t0, CHUNK), h * HD:(h + 1) * HD]
            delta_ref[part, :] = jnp.broadcast_to(row_ref[h:h + 1, pl.ds(t0, CHUNK)], (HD, CHUNK)).T
        small = jnp.max(row_ref[heads:, pl.ds(t0, CHUNK)]) * key_most * (to_log2 * to_log2) <= SAFE * SAFE
        low, high = jnp.int32(0), jnp.int32(0)
        begin = jnp.int32(0)
        begins = []
        for d in range(lengths_ref.shape[0]):
            low = jnp.where(first >= begin, begin, low)
            high = jnp.where(end - 1 >= begin, begin, high)
            begins.append(begin)
            begin = begin + lengths_ref[d]
        count = (end - low + TILE - 1) // TILE
        plain_end = jnp.maximum((end - high) // TILE, 1)
        edges = 1 + count - plain_end

        def edge_tile(m):
            return jnp.where(m == 0, 0, plain_end + m - 1)

        def allowed_of(key0):
            query_pos = first + lax.broadcasted_iota(jnp.int32, (CHUNK, TILE), 0)
            key_pos = key0 + lax.broadcasted_iota(jnp.int32, (CHUNK, TILE), 1)
            row_start = jnp.zeros((CHUNK, TILE), jnp.int32)
            for one in begins:
                row_start = jnp.where(query_pos >= one, one, row_start)
            return (key_pos >= row_start) & (key_pos <= query_pos)

        def tile_at(n):
            return pl.multiple_of(end - TILE * (n + 1) + CHUNK, CHUNK)

        def scores(key, p):
            return lax.dot_general(q_rows[p * pair:(p + 1) * pair, :], key, LAST,
                                   preferred_element_type=jnp.float32) * to_log2

        def hide(values, allowed, other):
            return jnp.concatenate([jnp.where(allowed, values[:CHUNK], other),
                                    jnp.where(allowed, values[CHUNK:], other)], axis=0)

        def find_top(n, _):
            key = kv_ref[pl.ds(tile_at(n), TILE), :HD]
            allowed = allowed_of(tile_at(n) - CHUNK)
            for p in range(pairs):
                part = slice(p * pair, (p + 1) * pair)
                s = hide(scores(key, p), allowed, NEG)
                top_ref[part, :] = jnp.maximum(top_ref[part, :], jnp.maximum(s[:, :HD], s[:, HD:]))
            return 0

        def weigh(n, masked, shifted):
            key = kv_ref[pl.ds(tile_at(n), TILE), :HD]
            allowed = allowed_of(tile_at(n) - CHUNK) if masked else None
            for p in range(pairs):
                part = slice(p * pair, (p + 1) * pair)
                s = scores(key, p)
                if shifted:
                    s = hide(s, allowed, NEG) - jnp.concatenate([top_ref[part, :], top_ref[part, :]], axis=1)
                e = jnp.exp2(s)
                if masked and not shifted:
                    e = hide(e, allowed, 0.0)
                sum_ref[part, :] += e[:, :HD] + e[:, HD:]
                e_ref[n, part, :] = e.astype(jnp.bfloat16)
            return 0

        sum_ref[...] = jnp.zeros_like(sum_ref)

        @pl.when(small)
        def _():
            lax.fori_loop(0, edges, lambda m, _: weigh(edge_tile(m), True, False), 0)
            twos = (plain_end - 1) // 2

            def two(m, _):
                weigh(1 + 2 * m, False, False)
                return weigh(2 + 2 * m, False, False)

            lax.fori_loop(0, twos, two, 0)
            lax.fori_loop(1 + 2 * twos, plain_end, lambda n, _: weigh(n, False, False), 0)

        @pl.when(jnp.logical_not(small))
        def _():
            top_ref[...] = jnp.full_like(top_ref, NEG)
            lax.fori_loop(0, count, find_top, 0)
            top_ref[...] = jnp.broadcast_to(jnp.max(top_ref[...], axis=1, keepdims=True), top_ref.shape)
            lax.fori_loop(0, count, lambda n, _: weigh(n, True, True), 0)

        for h in range(heads):
            part = slice(h * CHUNK, (h + 1) * CHUNK)
            inverse = jnp.broadcast_to(1.0 / jnp.sum(sum_ref[part, :], axis=1, keepdims=True), (CHUNK, HD))
            sum_ref[part, :] = inverse
            q_turned[:, part] = (q_rows[part, :].astype(jnp.float32) * inverse).astype(jnp.bfloat16).T
            do_turned[:, part] = (do_rows[part, :].astype(jnp.float32) * inverse).astype(jnp.bfloat16).T
        dq_acc[...] = jnp.zeros_like(dq_acc)

        def grad_step(n, ds_ref):
            at = tile_at(n)
            block = at // HD
            key = kv_ref[pl.ds(at, TILE), :HD]
            value = kv_ref[pl.ds(at, TILE), HD:]
            for p in range(pairs):
                part = slice(p * pair, (p + 1) * pair)
                dp = lax.dot_general(do_rows[part, :], value, LAST, preferred_element_type=jnp.float32)
                delta = delta_ref[part, :]
                ds_ref[part, :] = (e_ref[n, part, :].astype(jnp.float32)
                                   * (dp - jnp.concatenate([delta, delta], axis=1))).astype(jnp.bfloat16)
            dv = jnp.dot(do_turned[...], e_ref[n], preferred_element_type=jnp.float32)
            dv_acc[block] += dv[:, :HD]
            dv_acc[block + 1] += dv[:, HD:]
            dq_acc[...] += jnp.dot(ds_ref[...], key, preferred_element_type=jnp.float32)
            dk = jnp.dot(q_turned[...], ds_ref[...], preferred_element_type=jnp.float32)
            dk_acc[block] += dk[:, :HD]
            dk_acc[block + 1] += dk[:, HD:]
            return 0

        def grad_two(m, _):
            grad_step(2 * m, ds_ref)
            return grad_step(2 * m + 1, ds_other)

        lax.fori_loop(0, count // 2, grad_two, 0)
        lax.fori_loop(count // 2 * 2, count, lambda n, _: grad_step(n, ds_ref), 0)
        for h in range(heads):
            part = slice(h * CHUNK, (h + 1) * CHUNK)
            dq_ref[pl.ds(t0, CHUNK), h * HD:(h + 1) * HD] = (
                dq_acc[part, :] * (sum_ref[part, :] * scale)).astype(jnp.bfloat16)
        pltpu.make_async_copy(dq_ref.at[pl.ds(t0, CHUNK), :], dq_hbm.at[pl.ds(t0, CHUNK), :], store_sem.at[j]).start()
        return 0

    lax.fori_loop(0, chunks, one_chunk, 0)

    def write(i, _):
        at = pl.ds(pl.multiple_of(i * HD, HD), HD)
        dkv_ref[at, :HD] = (dk_acc[i + 1] * scale).astype(jnp.bfloat16).T
        dkv_ref[at, HD:] = dv_acc[i + 1].astype(jnp.bfloat16).T
        return 0

    stores = []
    for n in range(PIECES):
        lax.fori_loop(n * piece // HD, (n + 1) * piece // HD, write, 0, unroll=4)
        stores.append(pltpu.make_async_copy(dkv_ref.at[pl.ds(n * piece, piece), :],
                                            dkv_hbm.at[pl.ds(n * piece, piece), :], store_sem.at[chunks + n]))
        stores[-1].start()
    for j in range(chunks):
        part = pl.ds(j * CHUNK, CHUNK)
        pltpu.make_async_copy(dq_ref.at[part, :], dq_hbm.at[part, :], store_sem.at[j]).wait()
    for copy in stores:
        copy.wait()


def attention(starts, lengths, q, do, row_info, kv, longest=4608):
    total = kv.shape[0]
    rows = q.shape[1] // HD * CHUNK
    max_tiles = (longest + CHUNK) // TILE + 2
    bf = jnp.bfloat16
    vmem = pl.BlockSpec(memory_space=pltpu.VMEM)
    smem = pl.BlockSpec(memory_space=pltpu.SMEM)
    anywhere = pl.BlockSpec(memory_space=pl.ANY)
    return pl.pallas_call(
        functools.partial(attention_kernel, total),
        out_shape=[jax.ShapeDtypeStruct(q.shape, bf), jax.ShapeDtypeStruct(kv.shape, bf)],
        in_specs=[smem, smem, vmem] + [anywhere] * 3,
        out_specs=[anywhere] * 2,
        scratch_shapes=[
            pltpu.VMEM(q.shape, bf),
            pltpu.VMEM(q.shape, bf),
            pltpu.VMEM((total + CHUNK, 2 * HD), bf),
            pltpu.VMEM(q.shape, bf),
            pltpu.VMEM(kv.shape, bf),
            pltpu.SemaphoreType.DMA((PIECES + 2,)),
            pltpu.SemaphoreType.DMA((q.shape[0] // CHUNK + PIECES,)),
            pltpu.VMEM((max_tiles, rows, TILE), bf),
            pltpu.VMEM((rows, TILE), bf),
            pltpu.VMEM((rows, TILE), bf),
            pltpu.VMEM((rows, HD), bf),
            pltpu.VMEM((rows, HD), bf),
            pltpu.VMEM((HD, rows), bf),
            pltpu.VMEM((HD, rows), bf),
            pltpu.VMEM((rows, HD), jnp.float32),
            pltpu.VMEM((rows, HD), jnp.float32),
            pltpu.VMEM((rows, HD), jnp.float32),
            pltpu.VMEM((rows, HD), jnp.float32),
            pltpu.VMEM((total // HD + 1, HD, HD), jnp.float32),
            pltpu.VMEM((total // HD + 1, HD, HD), jnp.float32),
        ],
        compiler_params=pltpu.CompilerParams(vmem_limit_bytes=62 * 2**20),
        name="attention",
    )(starts, lengths, row_info, q, do, kv)


SIDE = 4
MESH = pl.DeviceIdType.MESH


def ring_place(axis, step):
    me = lax.axis_index("ctx")
    x, z = me // SIDE, me % SIDE
    if axis == 0:
        return lax.rem(x + step + 2 * SIDE, SIDE) * SIDE + z
    return x * SIDE + lax.rem(z + step + SIDE, SIDE)


def block_at(axis, first, second):
    me = lax.axis_index("ctx")
    x, z = me // SIDE, me % SIDE
    along, across = (first, second) if axis == 0 else (second, first)
    return lax.rem(x + along + SIDE, SIDE) * SIDE + lax.rem(z + across + SIDE, SIDE)


def greet(partners):
    barrier = pltpu.get_barrier_semaphore()
    for partner in partners:
        pl.semaphore_signal(barrier, inc=1, device_id=partner, device_id_type=MESH)
    pl.semaphore_wait(barrier, len(partners))


RELAY = ((1, 0), (-1, 1))


def collect_kernel(k_ref, v_ref, q_ref, out_grad_ref, outputs_ref, kv_hbm, q_out, out_grad_out, row_out,
                   kv_ref, k_vmem, v_vmem, q_vmem, out_grad_vmem, outputs_vmem, row_vmem, relay, local_sem, out_sem, send_sem, recv_sem):
    me = lax.axis_index("ctx")
    rows = k_ref.shape[0]
    half = rows // 2
    mid = half // 2
    quarter = rows // SIDE
    own = [
        pltpu.make_async_copy(k_ref, k_vmem, local_sem.at[0]),
        pltpu.make_async_copy(v_ref, v_vmem, local_sem.at[1]),
    ]
    kept = [
        pltpu.make_async_copy(q_ref, q_vmem, local_sem.at[2]),
        pltpu.make_async_copy(out_grad_ref, out_grad_vmem, local_sem.at[3]),
        pltpu.make_async_copy(outputs_ref, outputs_vmem, local_sem.at[4]),
    ]
    for copy in own + kept:
        copy.start()
    for copy in own:
        copy.wait()
    kv_ref[me, :, :HD] = k_vmem[...]
    kv_ref[me, :, HD:] = v_vmem[...]
    greet([{"ctx": ring_place(axis, step)} for axis, step in ((0, 1), (0, -1), (0, 2), (1, 1), (1, -1))])
    copies = {}

    def begin(name, number, place, src, dst):
        copy = pltpu.make_async_remote_copy(
            src_ref=src, dst_ref=dst, send_sem=send_sem.at[number], recv_sem=recv_sem.at[number],
            device_id={"ctx": ring_place(*place)}, device_id_type=MESH)
        copy.start()
        copies[name] = copy

    def pass_on(name, number, place, block, start, count):
        region = kv_ref.at[block, pl.ds(start, count), :]
        begin(name, number, place, region, region)

    def near(h, item, shift):
        axis = 0 if item == "line" else 1
        base = h * 20 + (0 if item == "line" else 4 + 4 * item)
        block = me if item == "line" else block_at(0, shift, 0)
        pass_on((h, item, 0), base, (axis, 1), block, h * half, half)
        pass_on((h, item, 1), base + 1, (axis, -1), block, h * half, half)

    def far(h, item, shift):
        axis = 0 if item == "line" else 1
        base = h * 20 + (0 if item == "line" else 4 + 4 * item)

        def block(step):
            return block_at(0, step, 0) if item == "line" else block_at(0, shift, step)

        copies[h, item, 0].wait_recv()
        pass_on((h, item, 2), base + 2, (axis, 1), block(-1), h * half, mid)
        copies[h, item, 1].wait_recv()
        pass_on((h, item, 3), base + 3, (axis, -1), block(1), h * half + mid, mid)

    stores = []

    def keep(block, h):
        region = pl.ds(h * half, half)
        stores.append(pltpu.make_async_copy(kv_ref.at[block, region, :], kv_hbm.at[block, region, :],
                                            out_sem.at[len(stores)]))
        stores[-1].start()

    shifts = (0, -1, 1, 2)
    pairs = ((q_ref, q_out), (out_grad_ref, out_grad_out))
    for h in (0, 1):
        near(h, "line", 0)
    for h in (0, 1):
        near(h, 0, shifts[0])
    for h in (0, 1):
        far(h, "line", 0)
        near(h, 1, shifts[1])
        near(h, 2, shifts[2])
    for n, (src, dst) in enumerate(pairs):
        for step, slot in RELAY:
            part = pl.ds(2 * quarter + slot * (quarter // 2), quarter // 2)
            begin(("relay", n, slot), 40 + 2 * n + slot, (0, step), src.at[part, :], relay.at[n, slot])
    for n, (src, dst) in enumerate(pairs):
        for j, step in ((1, 1), (3, -1)):
            part = pl.ds(j * quarter, quarter)
            begin(("move", n, j), 44 + 2 * n + j // 2, (0, step), src.at[part, :], dst.at[part, :])
    for copy in kept:
        copy.wait()
    stay = [
        pltpu.make_async_copy(q_vmem.at[pl.ds(0, quarter), :], q_out.at[pl.ds(0, quarter), :], local_sem.at[0]),
        pltpu.make_async_copy(out_grad_vmem.at[pl.ds(0, quarter), :], out_grad_out.at[pl.ds(0, quarter), :],
                              local_sem.at[1]),
    ]
    for copy in stay:
        copy.start()
    for h in (0, 1):
        for shift in (0, -1, 1):
            keep(block_at(0, shift, 0), h)
    heads = row_vmem.shape[0] // 2
    for head in range(heads):
        part = slice(head * HD, (head + 1) * HD)
        grad = out_grad_vmem[:, part].astype(jnp.float32)
        query = q_vmem[:, part].astype(jnp.float32)
        row_vmem[head:head + 1, :] = jnp.sum((grad * outputs_vmem[:, part].astype(jnp.float32)).T, axis=0, keepdims=True)
        row_vmem[heads + head:heads + head + 1, :] = jnp.sum((query * query).T, axis=0, keepdims=True)
    for j, step in ((1, 1), (2, 2), (3, -1)):
        part = pl.ds(j * quarter, quarter)
        begin(("rows", j), 51 + j, (0, step), row_vmem.at[:, part], row_out.at[:, part])
    row_out[:, :quarter] = row_vmem[:, :quarter]
    for h in (0, 1):
        far(h, 0, shifts[0])
        keep(block_at(0, 0, 1), h)
        keep(block_at(0, 0, -1), h)
    for h in (0, 1):
        copies[h, "line", 2].wait_recv()
        copies[h, "line", 3].wait_recv()
        near(h, 3, shifts[3])
        keep(block_at(0, 2, 0), h)
    for n, (src, dst) in enumerate(pairs):
        for step, slot in RELAY:
            part = pl.ds(2 * quarter + slot * (quarter // 2), quarter // 2)
            copies["relay", n, slot].wait_recv()
            begin(("relayed", n, slot), 48 + 2 * n + slot, (0, step), relay.at[n, slot], dst.at[part, :])
    for item in (1, 2, 3):
        for h in (0, 1):
            far(h, item, shifts[item])
            keep(block_at(0, shifts[item], 1), h)
            keep(block_at(0, shifts[item], -1), h)
    for item in (0, 1, 2, 3):
        for h in (0, 1):
            copies[h, item, 2].wait_recv()
            copies[h, item, 3].wait_recv()
            keep(block_at(0, shifts[item], 2), h)
    for n in (0, 1):
        for name in (("move", n, 1), ("move", n, 3), ("relayed", n, 0), ("relayed", n, 1)):
            copies[name].wait_recv()
    for j in (1, 2, 3):
        copies["rows", j].wait_recv()
    for copy in stay + stores:
        copy.wait()
    for copy in copies.values():
        copy.wait_send()


def collect(keys, values, queries, out_grad, outputs):
    rows = keys.shape[0]
    heads = out_grad.shape[1] // HD
    bf = jnp.bfloat16
    vmem = pl.BlockSpec(memory_space=pltpu.VMEM)
    anywhere = pl.BlockSpec(memory_space=pl.ANY)
    return pl.pallas_call(
        collect_kernel,
        out_shape=[jax.ShapeDtypeStruct((SIDE * SIDE, rows, 2 * HD), bf),
                   jax.ShapeDtypeStruct(queries.shape, bf),
                   jax.ShapeDtypeStruct(queries.shape, bf),
                   jax.ShapeDtypeStruct((2 * heads, rows), jnp.float32)],
        in_specs=[anywhere] * 5,
        out_specs=[anywhere] * 3 + [vmem],
        scratch_shapes=[pltpu.VMEM((SIDE * SIDE, rows, 2 * HD), bf), pltpu.VMEM(keys.shape, bf), pltpu.VMEM(keys.shape, bf), pltpu.VMEM(queries.shape, bf), pltpu.VMEM(queries.shape, bf), pltpu.VMEM(queries.shape, bf),
                        pltpu.VMEM((2 * heads, rows), jnp.float32),
                        pltpu.VMEM((2, 2, rows // SIDE // 2, queries.shape[1]), bf),
                        pltpu.SemaphoreType.DMA((5,)), pltpu.SemaphoreType.DMA((2 * SIDE * SIDE,)), pltpu.SemaphoreType.DMA((55,)), pltpu.SemaphoreType.DMA((55,))],
        compiler_params=pltpu.CompilerParams(collective_id=0, has_side_effects=True, vmem_limit_bytes=62 * 2**20),
        name="collect",
    )(keys, values, queries, out_grad, outputs)


PARTS = 4
PART_ORDER = (0, 1, 3, 2)
FIRST_AXIS = ((0, 0), (0, 0), (0, 1), (0, 1))
RS_ORDER = (2, -1, 1, 0)


def tp_place(step, core):
    y = lax.axis_index("tp") // 2
    return lax.rem(y + step + SIDE, SIDE) * 2 + core


def finish_kernel(dq_in, dkv_hbm, wq_hbm, wk_hbm, wv_hbm, out_ref, dkv_ref, dq_ref, relay, wq_ref, wk_ref, wv_ref, wkv_ref, acc_ref, sum_ref,
                  low_ref, high_ref, stage_ref, fin_ref, res_ref, pair_out, pair_in, y_stage, y_low, y_high, y_fin,
                  load_sem, send_sem, recv_sem):
    core = lax.axis_index("tp") % 2
    rows = dq_ref.shape[0]
    part_rows = rows // PARTS
    size = part_rows // 2
    mid = size // 2
    loads = [
        pltpu.make_async_copy(dkv_hbm, dkv_ref, load_sem.at[0]),
        pltpu.make_async_copy(wq_hbm, wq_ref, load_sem.at[1]),
        pltpu.make_async_copy(wk_hbm, wk_ref, load_sem.at[2]),
        pltpu.make_async_copy(wv_hbm, wv_ref, load_sem.at[3]),
        pltpu.make_async_copy(dq_in.at[pl.ds(0, part_rows), :], dq_ref.at[pl.ds(0, part_rows), :], load_sem.at[4]),
    ]
    for copy in loads:
        copy.start()
    greet([{"ctx": ring_place(axis, step)} for axis in (0, 1) for step in (1, -1)]
          + [{"tp": tp_place(step, core)} for step in (1, -1)] + [{"tp": tp_place(0, 1 - core)}])
    copies = {}

    def begin(name, number, device, src, dst):
        copy = pltpu.make_async_remote_copy(src_ref=src, dst_ref=dst, send_sem=send_sem.at[number],
                                            recv_sem=recv_sem.at[number], device_id=device, device_id_type=MESH)
        copy.start()
        copies[name] = copy

    def wide(value):
        return value.astype(jnp.float32)

    def rows_of(s, h):
        return pl.ds(s * part_rows + h * size, size)

    def ident(s, h, k):
        return (s * 2 + h) * 5 + (4 if k is None else RS_ORDER.index(k))

    def term(s, h, k, shift, start, count):
        if k is None:
            return res_ref.at[s, h, RS_ORDER.index(shift), pl.ds(start, count), :]
        return dkv_ref.at[block_at(FIRST_AXIS[s][h], k, shift), pl.ds(s * part_rows + h * size + start, count), :]

    def ring_axis(s, h, k):
        return FIRST_AXIS[s][h] if k is None else 1 - FIRST_AXIS[s][h]

    def reduce_send(s, h, k):
        n, axis = ident(s, h, k), ring_axis(s, h, k)
        begin(("low", n), 4 * n, {"ctx": ring_place(axis, 1)}, term(s, h, k, 2, 0, mid), low_ref.at[n])
        begin(("high", n), 4 * n + 1, {"ctx": ring_place(axis, -1)}, term(s, h, k, 2, mid, mid), high_ref.at[n])

    def reduce_pass(s, h, k):
        n, axis = ident(s, h, k), ring_axis(s, h, k)
        copies["low", n].wait_recv()
        stage_ref[n, 0, :mid, :] = (wide(term(s, h, k, 1, 0, mid)[...]) + wide(low_ref[n])).astype(jnp.bfloat16)
        stage_ref[n, 0, mid:, :] = term(s, h, k, 1, mid, mid)[...]
        begin(("up", n), 4 * n + 2, {"ctx": ring_place(axis, 1)}, stage_ref.at[n, 0], fin_ref.at[n, 0])
        copies["high", n].wait_recv()
        stage_ref[n, 1, :mid, :] = term(s, h, k, -1, 0, mid)[...]
        stage_ref[n, 1, mid:, :] = (wide(term(s, h, k, -1, mid, mid)[...]) + wide(high_ref[n])).astype(jnp.bfloat16)
        begin(("down", n), 4 * n + 3, {"ctx": ring_place(axis, -1)}, stage_ref.at[n, 1], fin_ref.at[n, 1])

    def reduce_end(s, h, k):
        n = ident(s, h, k)
        copies["up", n].wait_recv()
        copies["down", n].wait_recv()
        total = wide(term(s, h, k, 0, 0, size)[...]) + wide(fin_ref[n, 0]) + wide(fin_ref[n, 1])
        if k is None:
            sum_ref[rows_of(s, h), :] = total.astype(jnp.bfloat16)
        else:
            res_ref[s, h, RS_ORDER.index(k)] = total.astype(jnp.bfloat16)

    def reduce_steps(s):
        for k in RS_ORDER:
            for h in (0, 1):
                reduce_send(s, h, k)
        yield
        for k in RS_ORDER:
            for h in (0, 1):
                reduce_pass(s, h, k)
        yield
        for h in (0, 1):
            reduce_end(s, h, 2)
            reduce_send(s, h, None)
        yield
        for h in (0, 1):
            reduce_end(s, h, -1)
            reduce_end(s, h, 1)
        for h in (0, 1):
            reduce_pass(s, h, None)
        yield
        for h in (0, 1):
            reduce_end(s, h, 0)
        yield
        for h in (0, 1):
            reduce_end(s, h, None)
        yield

    def project(g, n):
        part = pl.ds(n * (rows // 2), rows // 2)
        acc_ref[g, part, :] = lax.dot_general(dq_ref[part, :], wq_ref[g], LAST, preferred_element_type=jnp.float32)

    back = 48 * PARTS

    def give_back():
        for step, slot in RELAY:
            part = pl.ds(2 * part_rows + slot * size, size)
            begin(("relay", slot), back + slot, {"ctx": ring_place(0, step)}, dq_in.at[part, :], relay.at[slot])
        for j, step in ((1, -1), (3, 1)):
            part = pl.ds(j * part_rows, part_rows)
            begin(("back", j), back + 2 + j // 2, {"ctx": ring_place(0, step)}, dq_in.at[part, :], dq_ref.at[part, :])

    def relay_back():
        for step, slot in RELAY:
            part = pl.ds(2 * part_rows + slot * size, size)
            copies["relay", slot].wait_recv()
            begin(("relayed", slot), back + 4 + slot, {"ctx": ring_place(0, step)}, relay.at[slot], dq_ref.at[part, :])

    far = 40 * PARTS

    def spread(s, step):
        n = s * 4 + RS_ORDER.index(step)
        other, mine = tp_place(step, 1 - core), tp_place(step, core)
        part = pl.ds(s * part_rows, part_rows)
        low = sum_ref[part, :]
        total = acc_ref[other, part, :] + lax.dot_general(low, wkv_ref[other], LAST, preferred_element_type=jnp.float32)
        pair_out[n, 0] = total[:size].astype(jnp.bfloat16)
        pair_out[n, 1] = total[size:].astype(jnp.bfloat16)
        begin(("pair", n), far + n, {"tp": tp_place(0, 1 - core)}, pair_out.at[n], pair_in.at[n])
        acc_ref[mine, part, :] += lax.dot_general(low, wkv_ref[mine], LAST, preferred_element_type=jnp.float32)

    def chip_sum(s, step, h):
        n = s * 4 + RS_ORDER.index(step)
        return acc_ref[tp_place(step, core), rows_of(s, h), :] + wide(pair_in[n, h])

    def y_send(s):
        copies["pair", s * 4].wait_recv()
        for h in (0, 1):
            y_stage[s, 0, h] = chip_sum(s, 2, h).astype(jnp.bfloat16)
        number = far + 4 * PARTS + 4 * s
        begin(("y_low", s), number, {"tp": tp_place(1, core)}, y_stage.at[s, 0, 0], y_low.at[s])
        begin(("y_high", s), number + 1, {"tp": tp_place(-1, core)}, y_stage.at[s, 0, 1], y_high.at[s])

    def y_pass(s, step):
        number = far + 4 * PARTS + 4 * s
        copies["pair", s * 4 + RS_ORDER.index(step)].wait_recv()
        slot, low = (1, 0) if step == 1 else (2, 1)
        y_stage[s, slot, 1 - low] = chip_sum(s, step, 1 - low).astype(jnp.bfloat16)
        copies["y_low" if step == 1 else "y_high", s].wait_recv()
        came = y_low if step == 1 else y_high
        y_stage[s, slot, low] = (chip_sum(s, step, low) + wide(came[s])).astype(jnp.bfloat16)
        begin(("y_fin", s, step), number + 1 + slot, {"tp": tp_place(step, core)}, y_stage.at[s, slot],
              y_fin.at[s, slot - 1])

    def y_end(s):
        copies["pair", s * 4 + 3].wait_recv()
        copies["y_fin", s, 1].wait_recv()
        copies["y_fin", s, -1].wait_recv()
        for h in (0, 1):
            out_ref[rows_of(s, h), :] = (
                chip_sum(s, 0, h) + wide(y_fin[s, 0, h]) + wide(y_fin[s, 1, h])).astype(jnp.bfloat16)

    sums = {s: reduce_steps(s) for s in PART_ORDER}
    one, two, three, four = PART_ORDER
    loads[0].wait()
    next(sums[one])
    next(sums[two])
    give_back()
    next(sums[one])
    next(sums[three])
    next(sums[two])
    next(sums[one])
    relay_back()
    next(sums[one])
    loads[1].wait()
    loads[4].wait()
    copies["back", 1].wait_recv()
    for g in range(0, 4):
        project(g, 0)
    next(sums[one])
    next(sums[two])
    next(sums[three])
    next(sums[four])
    for g in range(4, 8):
        project(g, 0)
    loads[2].wait()
    loads[3].wait()

    def merge(g, _):
        wkv_ref[g, :, :HD] = wk_ref[g]
        wkv_ref[g, :, HD:] = wv_ref[g]
        return 0

    lax.fori_loop(0, wkv_ref.shape[0], merge, 0)
    next(sums[one])
    next(sums[two])
    for step in (2, 1):
        spread(one, step)
    next(sums[two])
    next(sums[three])
    next(sums[four])
    y_send(one)
    for step in (-1, 0):
        spread(one, step)
    copies["back", 3].wait_recv()
    copies["relayed", 0].wait_recv()
    copies["relayed", 1].wait_recv()
    for g in range(0, 4):
        project(g, 1)
    next(sums[two])
    next(sums[three])
    y_pass(one, 1)
    y_pass(one, -1)
    for step in RS_ORDER:
        spread(two, step)
    next(sums[four])
    next(sums[three])
    y_send(two)
    for g in range(4, 8):
        project(g, 1)
    next(sums[three])
    next(sums[four])
    y_pass(two, 1)
    y_pass(two, -1)
    for step in RS_ORDER:
        spread(three, step)
    next(sums[four])
    y_send(three)
    next(sums[four])
    for step in RS_ORDER:
        spread(four, step)
    y_end(one)
    y_pass(three, 1)
    y_pass(three, -1)
    y_send(four)
    y_end(two)
    y_pass(four, 1)
    y_pass(four, -1)
    y_end(three)
    y_end(four)
    for copy in copies.values():
        copy.wait_send()


def finish(query_grad, terms, w_query, w_key, w_value):
    rows = query_grad.shape[0]
    blocks = SIDE * 2
    columns = w_query.shape[0] // blocks
    size = rows // PARTS // 2
    mid = size // 2
    reduces = 10 * PARTS
    sems = 4 * reduces + 8 * PARTS + 6
    bf = jnp.bfloat16
    vmem = pl.BlockSpec(memory_space=pltpu.VMEM)
    anywhere = pl.BlockSpec(memory_space=pl.ANY)
    return pl.pallas_call(
        finish_kernel,
        out_shape=jax.ShapeDtypeStruct((rows, columns), bf),
        in_specs=[anywhere] * 5,
        out_specs=vmem,
        scratch_shapes=[
            pltpu.VMEM(terms.shape, bf),
            pltpu.VMEM(query_grad.shape, bf),
            pltpu.VMEM((2, size, query_grad.shape[1]), bf),
            pltpu.VMEM((blocks, columns, w_query.shape[1]), bf),
            pltpu.VMEM((blocks, columns, HD), bf),
            pltpu.VMEM((blocks, columns, HD), bf),
            pltpu.VMEM((blocks, columns, 2 * HD), bf),
            pltpu.VMEM((blocks, rows, columns), jnp.float32),
            pltpu.VMEM((rows, 2 * HD), bf),
            pltpu.VMEM((reduces, mid, 2 * HD), bf),
            pltpu.VMEM((reduces, mid, 2 * HD), bf),
            pltpu.VMEM((reduces, 2, size, 2 * HD), bf),
            pltpu.VMEM((reduces, 2, size, 2 * HD), bf),
            pltpu.VMEM((PARTS, 2, 4, size, 2 * HD), bf),
            pltpu.VMEM((4 * PARTS, 2, size, columns), bf),
            pltpu.VMEM((4 * PARTS, 2, size, columns), bf),
            pltpu.VMEM((PARTS, 3, 2, size, columns), bf),
            pltpu.VMEM((PARTS, size, columns), bf),
            pltpu.VMEM((PARTS, size, columns), bf),
            pltpu.VMEM((PARTS, 2, 2, size, columns), bf),
            pltpu.SemaphoreType.DMA((5,)),
            pltpu.SemaphoreType.DMA((sems,)),
            pltpu.SemaphoreType.DMA((sems,)),
        ],
        compiler_params=pltpu.CompilerParams(collective_id=1, has_side_effects=True, vmem_limit_bytes=62 * 2**20),
        name="finish",
    )(query_grad, terms, w_query.reshape(blocks, columns, -1), w_key.reshape(blocks, columns, -1),
      w_value.reshape(blocks, columns, -1))


def shards(queries, keys, values, outputs, out_grad, lengths, w_query, w_key, w_value):
    rows = queries.shape[0]
    starts = jnp.stack([ring_place(0, -j) * rows + j * CHUNK for j in range(SIDE)]).astype(jnp.int32)
    collected, q_work, grad_work, row_info = collect(keys, values, queries, out_grad, outputs)
    query_grad, terms = attention(starts, lengths, q_work, grad_work, row_info, collected.reshape(-1, 2 * HD))
    return finish(query_grad, terms.reshape(collected.shape), w_query, w_key, w_value)


def solution(mesh):
    in_specs = (P("ctx", "tp"),) * 5 + (P(),) + (P(None, "tp"),) * 3
    return jax.shard_map(shards, mesh=mesh, in_specs=in_specs, out_specs=P("ctx", "tp"), check_vma=False)
```

```python
import functools
import jax, jax.numpy as jnp
from jax import lax
from jax.experimental import pallas as pl
from jax.experimental.pallas import tpu as pltpu
from jax.sharding import PartitionSpec as P

HD = 128
CHUNK = 128
TILE = 256
NEG = -1e30
SAFE = 60.0
LAST = (((1,), (1,)), ((), ()))
PIECES = 4


def attention_kernel(total, lengths_ref, row_ref, q_hbm, do_hbm, kv_hbm, dq_hbm, dkv_hbm,
                     q_ref, do_ref, kv_ref, dq_ref, dkv_ref, load_sem, store_sem, e_ref, ds_ref, ds_other, ds_third, q_rows, do_rows,
                     q_turned, do_turned, delta_ref, top_ref, sum_ref, dq_acc, dk_acc, dv_acc):
    rows = q_rows.shape[0]
    heads = rows // CHUNK
    pair = 2 * CHUNK
    pairs = rows // pair
    chunks = q_ref.shape[0] // CHUNK
    blocks = total // HD
    scale = HD ** -0.5
    to_log2 = scale * 1.4426950408889634
    piece = total // PIECES
    loads = [pltpu.make_async_copy(kv_hbm.at[pl.ds(n * piece, piece), :],
                                   kv_ref.at[pl.ds(CHUNK + n * piece, piece), :], load_sem.at[n])
             for n in range(PIECES)]
    loads += [pltpu.make_async_copy(q_hbm, q_ref, load_sem.at[PIECES]),
              pltpu.make_async_copy(do_hbm, do_ref, load_sem.at[PIECES + 1])]
    for copy in loads:
        copy.start()
    kv_ref[:CHUNK, :] = jnp.zeros((CHUNK, 2 * HD), jnp.bfloat16)

    def clear(i, _):
        dk_acc[i] = jnp.zeros((HD, HD), jnp.float32)
        dv_acc[i] = jnp.zeros((HD, HD), jnp.float32)
        return 0

    lax.fori_loop(0, blocks + 1, clear, 0)

    def measure_keys(i, most):
        wide = kv_ref[pl.ds(pl.multiple_of(CHUNK + i * TILE, CHUNK), TILE), :HD].astype(jnp.float32)
        return jnp.maximum(most, jnp.sum(wide * wide, axis=1, keepdims=True))

    key_most = jnp.zeros((TILE, 1), jnp.float32)
    for n in range(PIECES):
        loads[n].wait()
        key_most = lax.fori_loop(n * piece // TILE, (n + 1) * piece // TILE, measure_keys, key_most)
    key_most = jnp.max(key_most)
    for copy in loads[PIECES:]:
        copy.wait()

    def one_chunk(j, _):
        first = work_start(j, chunks * CHUNK)
        end = first + CHUNK
        t0 = pl.multiple_of(j * CHUNK, CHUNK)
        for h in range(heads):
            part = slice(h * CHUNK, (h + 1) * CHUNK)
            q_rows[part, :] = q_ref[pl.ds(t0, CHUNK), h * HD:(h + 1) * HD]
            do_rows[part, :] = do_ref[pl.ds(t0, CHUNK), h * HD:(h + 1) * HD]
            delta_ref[part, :] = jnp.broadcast_to(row_ref[h:h + 1, pl.ds(t0, CHUNK)], (HD, CHUNK)).T
        small = jnp.max(row_ref[heads:, pl.ds(t0, CHUNK)]) * key_most * (to_log2 * to_log2) <= SAFE * SAFE
        low, high = jnp.int32(0), jnp.int32(0)
        begin = jnp.int32(0)
        begins = []
        for d in range(lengths_ref.shape[0]):
            low = jnp.where(first >= begin, begin, low)
            high = jnp.where(end - 1 >= begin, begin, high)
            begins.append(begin)
            begin = begin + lengths_ref[d]
        count = (end - low + TILE - 1) // TILE
        plain_end = jnp.maximum((end - high) // TILE, 1)
        edges = 1 + count - plain_end

        def edge_tile(m):
            return jnp.where(m == 0, 0, plain_end + m - 1)

        def allowed_of(key0):
            query_pos = first + lax.broadcasted_iota(jnp.int32, (CHUNK, TILE), 0)
            key_pos = key0 + lax.broadcasted_iota(jnp.int32, (CHUNK, TILE), 1)
            row_start = jnp.zeros((CHUNK, TILE), jnp.int32)
            for one in begins:
                row_start = jnp.where(query_pos >= one, one, row_start)
            return (key_pos >= row_start) & (key_pos <= query_pos)

        def tile_at(n):
            return pl.multiple_of(end - TILE * (n + 1) + CHUNK, CHUNK)

        def scores(key, p):
            return lax.dot_general(q_rows[p * pair:(p + 1) * pair, :], key, LAST,
                                   preferred_element_type=jnp.float32) * to_log2

        def hide(values, allowed, other):
            return jnp.concatenate([jnp.where(allowed, values[:CHUNK], other),
                                    jnp.where(allowed, values[CHUNK:], other)], axis=0)

        def find_top(n, _):
            key = kv_ref[pl.ds(tile_at(n), TILE), :HD]
            allowed = allowed_of(tile_at(n) - CHUNK)
            for p in range(pairs):
                part = slice(p * pair, (p + 1) * pair)
                s = hide(scores(key, p), allowed, NEG)
                top_ref[part, :] = jnp.maximum(top_ref[part, :], jnp.maximum(s[:, :HD], s[:, HD:]))
            return 0

        def weigh(n, masked, shifted):
            key = kv_ref[pl.ds(tile_at(n), TILE), :HD]
            allowed = allowed_of(tile_at(n) - CHUNK) if masked else None
            for p in range(pairs):
                part = slice(p * pair, (p + 1) * pair)
                s = scores(key, p)
                if shifted:
                    s = hide(s, allowed, NEG) - jnp.concatenate([top_ref[part, :], top_ref[part, :]], axis=1)
                e = jnp.exp2(s)
                if masked and not shifted:
                    e = hide(e, allowed, 0.0)
                sum_ref[part, :] += e[:, :HD] + e[:, HD:]
                e_ref[n, part, :] = e.astype(jnp.bfloat16)
            return 0

        sum_ref[...] = jnp.zeros_like(sum_ref)

        @pl.when(small)
        def _():
            lax.fori_loop(0, edges, lambda m, _: weigh(edge_tile(m), True, False), 0)
            fours = (plain_end - 1) // 4

            def four(m, _):
                for u in range(4):
                    weigh(1 + 4 * m + u, False, False)
                return 0

            lax.fori_loop(0, fours, four, 0)
            lax.fori_loop(1 + 4 * fours, plain_end, lambda n, _: weigh(n, False, False), 0)

        @pl.when(jnp.logical_not(small))
        def _():
            top_ref[...] = jnp.full_like(top_ref, NEG)
            lax.fori_loop(0, count, find_top, 0)
            top_ref[...] = jnp.broadcast_to(jnp.max(top_ref[...], axis=1, keepdims=True), top_ref.shape)
            lax.fori_loop(0, count, lambda n, _: weigh(n, True, True), 0)

        for h in range(heads):
            part = slice(h * CHUNK, (h + 1) * CHUNK)
            inverse = jnp.broadcast_to(1.0 / jnp.sum(sum_ref[part, :], axis=1, keepdims=True), (CHUNK, HD))
            sum_ref[part, :] = inverse
            q_turned[:, part] = (q_rows[part, :].astype(jnp.float32) * inverse).astype(jnp.bfloat16).T
            do_turned[:, part] = (do_rows[part, :].astype(jnp.float32) * inverse).astype(jnp.bfloat16).T
        dq_acc[...] = jnp.zeros_like(dq_acc)

        def grad_step(n, ds_ref):
            at = tile_at(n)
            block = at // HD
            key = kv_ref[pl.ds(at, TILE), :HD]
            value = kv_ref[pl.ds(at, TILE), HD:]
            for p in range(pairs):
                part = slice(p * pair, (p + 1) * pair)
                dp = lax.dot_general(do_rows[part, :], value, LAST, preferred_element_type=jnp.float32)
                delta = delta_ref[part, :]
                ds_ref[part, :] = (e_ref[n, part, :].astype(jnp.float32)
                                   * (dp - jnp.concatenate([delta, delta], axis=1))).astype(jnp.bfloat16)
            dv = jnp.dot(do_turned[...], e_ref[n], preferred_element_type=jnp.float32)
            dv_acc[block] += dv[:, :HD]
            dv_acc[block + 1] += dv[:, HD:]
            dq_acc[...] += jnp.dot(ds_ref[...], key, preferred_element_type=jnp.float32)
            dk = jnp.dot(q_turned[...], ds_ref[...], preferred_element_type=jnp.float32)
            dk_acc[block] += dk[:, :HD]
            dk_acc[block + 1] += dk[:, HD:]
            return 0

        def grad_three(m, _):
            grad_step(3 * m, ds_ref)
            grad_step(3 * m + 1, ds_other)
            return grad_step(3 * m + 2, ds_third)

        lax.fori_loop(0, count // 3, grad_three, 0)
        lax.fori_loop(count // 3 * 3, count, lambda n, _: grad_step(n, ds_ref), 0)
        for h in range(heads):
            part = slice(h * CHUNK, (h + 1) * CHUNK)
            dq_ref[pl.ds(t0, CHUNK), h * HD:(h + 1) * HD] = (
                dq_acc[part, :] * (sum_ref[part, :] * scale)).astype(jnp.bfloat16)
        pltpu.make_async_copy(dq_ref.at[pl.ds(t0, CHUNK), :], dq_hbm.at[pl.ds(t0, CHUNK), :], store_sem.at[j]).start()
        return 0

    lax.fori_loop(0, chunks, one_chunk, 0)

    def write(i, _):
        at = pl.ds(pl.multiple_of(i * HD, HD), HD)
        dkv_ref[at, :HD] = (dk_acc[i + 1] * scale).astype(jnp.bfloat16).T
        dkv_ref[at, HD:] = dv_acc[i + 1].astype(jnp.bfloat16).T
        return 0

    stores = []
    for n in range(PIECES):
        lax.fori_loop(n * piece // HD, (n + 1) * piece // HD, write, 0, unroll=4)
        stores.append(pltpu.make_async_copy(dkv_ref.at[pl.ds(n * piece, piece), :],
                                            dkv_hbm.at[pl.ds(n * piece, piece), :], store_sem.at[chunks + n]))
        stores[-1].start()
    for j in range(chunks):
        part = pl.ds(j * CHUNK, CHUNK)
        pltpu.make_async_copy(dq_ref.at[part, :], dq_hbm.at[part, :], store_sem.at[j]).wait()
    for copy in stores:
        copy.wait()


def attention(lengths, q, do, row_info, kv, longest=4608):
    total = kv.shape[0]
    rows = q.shape[1] // HD * CHUNK
    max_tiles = (longest + CHUNK) // TILE + 2
    bf = jnp.bfloat16
    vmem = pl.BlockSpec(memory_space=pltpu.VMEM)
    smem = pl.BlockSpec(memory_space=pltpu.SMEM)
    anywhere = pl.BlockSpec(memory_space=pl.ANY)
    return pl.pallas_call(
        functools.partial(attention_kernel, total),
        out_shape=[jax.ShapeDtypeStruct(q.shape, bf), jax.ShapeDtypeStruct(kv.shape, bf)],
        in_specs=[smem, vmem] + [anywhere] * 3,
        out_specs=[anywhere] * 2,
        scratch_shapes=[
            pltpu.VMEM(q.shape, bf),
            pltpu.VMEM(q.shape, bf),
            pltpu.VMEM((total + CHUNK, 2 * HD), bf),
            pltpu.VMEM(q.shape, bf),
            pltpu.VMEM(kv.shape, bf),
            pltpu.SemaphoreType.DMA((PIECES + 2,)),
            pltpu.SemaphoreType.DMA((q.shape[0] // CHUNK + PIECES,)),
            pltpu.VMEM((max_tiles, rows, TILE), bf),
            pltpu.VMEM((rows, TILE), bf),
            pltpu.VMEM((rows, TILE), bf),
            pltpu.VMEM((rows, TILE), bf),
            pltpu.VMEM((rows, HD), bf),
            pltpu.VMEM((rows, HD), bf),
            pltpu.VMEM((HD, rows), bf),
            pltpu.VMEM((HD, rows), bf),
            pltpu.VMEM((rows, HD), jnp.float32),
            pltpu.VMEM((rows, HD), jnp.float32),
            pltpu.VMEM((rows, HD), jnp.float32),
            pltpu.VMEM((rows, HD), jnp.float32),
            pltpu.VMEM((total // HD + 1, HD, HD), jnp.float32),
            pltpu.VMEM((total // HD + 1, HD, HD), jnp.float32),
        ],
        compiler_params=pltpu.CompilerParams(vmem_limit_bytes=62 * 2**20),
        name="attention",
    )(lengths, row_info, q, do, kv)


SIDE = 4
MESH = pl.DeviceIdType.MESH


def ring_place(axis, step):
    me = lax.axis_index("ctx")
    x, z = me // SIDE, me % SIDE
    if axis == 0:
        return lax.rem(x + step + 2 * SIDE, SIDE) * SIDE + z
    return x * SIDE + lax.rem(z + step + SIDE, SIDE)


def block_at(axis, first, second):
    me = lax.axis_index("ctx")
    x, z = me // SIDE, me % SIDE
    along, across = (first, second) if axis == 0 else (second, first)
    return lax.rem(x + along + SIDE, SIDE) * SIDE + lax.rem(z + across + SIDE, SIDE)


def greet(partners):
    barrier = pltpu.get_barrier_semaphore()
    for partner in partners:
        pl.semaphore_signal(barrier, inc=1, device_id=partner, device_id_type=MESH)
    pl.semaphore_wait(barrier, len(partners))


RELAY = ((1, 0), (-1, 1))


def collect_kernel(k_ref, v_ref, q_ref, out_grad_ref, outputs_ref, kv_hbm, q_out, out_grad_out, row_out,
                   kv_ref, k_vmem, v_vmem, q_vmem, out_grad_vmem, outputs_vmem, row_vmem, relay, local_sem, out_sem, send_sem, recv_sem):
    me = lax.axis_index("ctx")
    rows = k_ref.shape[0]
    half = rows // 2
    mid = half // 2
    quarter = rows // SIDE
    own = [
        pltpu.make_async_copy(k_ref, k_vmem, local_sem.at[0]),
        pltpu.make_async_copy(v_ref, v_vmem, local_sem.at[1]),
    ]
    kept = [
        pltpu.make_async_copy(q_ref, q_vmem, local_sem.at[2]),
        pltpu.make_async_copy(out_grad_ref, out_grad_vmem, local_sem.at[3]),
        pltpu.make_async_copy(outputs_ref, outputs_vmem, local_sem.at[4]),
    ]
    for copy in own + kept:
        copy.start()
    for copy in own:
        copy.wait()
    kv_ref[me, :, :HD] = k_vmem[...]
    kv_ref[me, :, HD:] = v_vmem[...]
    greet([{"ctx": ring_place(axis, step)} for axis, step in ((0, 1), (0, -1), (0, 2), (1, 1), (1, -1))])
    copies = {}

    def begin(name, number, place, src, dst):
        copy = pltpu.make_async_remote_copy(
            src_ref=src, dst_ref=dst, send_sem=send_sem.at[number], recv_sem=recv_sem.at[number],
            device_id={"ctx": ring_place(*place)}, device_id_type=MESH)
        copy.start()
        copies[name] = copy

    def pass_on(name, number, place, block, start, count):
        region = kv_ref.at[block, pl.ds(start, count), :]
        begin(name, number, place, region, region)

    def near(h, item, shift):
        axis = 0 if item == "line" else 1
        base = h * 20 + (0 if item == "line" else 4 + 4 * item)
        block = me if item == "line" else block_at(0, shift, 0)
        pass_on((h, item, 0), base, (axis, 1), block, h * half, half)
        pass_on((h, item, 1), base + 1, (axis, -1), block, h * half, half)

    def far(h, item, shift):
        axis = 0 if item == "line" else 1
        base = h * 20 + (0 if item == "line" else 4 + 4 * item)

        def block(step):
            return block_at(0, step, 0) if item == "line" else block_at(0, shift, step)

        copies[h, item, 0].wait_recv()
        pass_on((h, item, 2), base + 2, (axis, 1), block(-1), h * half, mid)
        copies[h, item, 1].wait_recv()
        pass_on((h, item, 3), base + 3, (axis, -1), block(1), h * half + mid, mid)

    stores = []

    def keep(block, h):
        region = pl.ds(h * half, half)
        stores.append(pltpu.make_async_copy(kv_ref.at[block, region, :], kv_hbm.at[block, region, :],
                                            out_sem.at[len(stores)]))
        stores[-1].start()

    shifts = (0, -1, 1, 2)
    pairs = ((q_ref, q_out), (out_grad_ref, out_grad_out))
    for h in (0, 1):
        near(h, "line", 0)
    for h in (0, 1):
        near(h, 0, shifts[0])
    for h in (0, 1):
        far(h, "line", 0)
        near(h, 1, shifts[1])
        near(h, 2, shifts[2])
    for n, (src, dst) in enumerate(pairs):
        for step, slot in RELAY:
            part = pl.ds(2 * quarter + slot * (quarter // 2), quarter // 2)
            begin(("relay", n, slot), 40 + 2 * n + slot, (0, step), src.at[part, :], relay.at[n, slot])
    for n, (src, dst) in enumerate(pairs):
        for j, step in ((1, 1), (3, -1)):
            part = pl.ds(j * quarter, quarter)
            begin(("move", n, j), 44 + 2 * n + j // 2, (0, step), src.at[part, :], dst.at[part, :])
    for copy in kept:
        copy.wait()
    stay = [
        pltpu.make_async_copy(q_vmem.at[pl.ds(0, quarter), :], q_out.at[pl.ds(0, quarter), :], local_sem.at[0]),
        pltpu.make_async_copy(out_grad_vmem.at[pl.ds(0, quarter), :], out_grad_out.at[pl.ds(0, quarter), :],
                              local_sem.at[1]),
    ]
    for copy in stay:
        copy.start()
    for h in (0, 1):
        for shift in (0, -1, 1):
            keep(block_at(0, shift, 0), h)
    heads = row_vmem.shape[0] // 2
    for head in range(heads):
        part = slice(head * HD, (head + 1) * HD)
        grad = out_grad_vmem[:, part].astype(jnp.float32)
        query = q_vmem[:, part].astype(jnp.float32)
        row_vmem[head:head + 1, :] = jnp.sum((grad * outputs_vmem[:, part].astype(jnp.float32)).T, axis=0, keepdims=True)
        row_vmem[heads + head:heads + head + 1, :] = jnp.sum((query * query).T, axis=0, keepdims=True)
    for j, step in ((1, 1), (2, 2), (3, -1)):
        part = pl.ds(j * quarter, quarter)
        begin(("rows", j), 51 + j, (0, step), row_vmem.at[:, part], row_out.at[:, part])
    row_out[:, :quarter] = row_vmem[:, :quarter]
    for h in (0, 1):
        far(h, 0, shifts[0])
        keep(block_at(0, 0, 1), h)
        keep(block_at(0, 0, -1), h)
    for h in (0, 1):
        copies[h, "line", 2].wait_recv()
        copies[h, "line", 3].wait_recv()
        near(h, 3, shifts[3])
        keep(block_at(0, 2, 0), h)
    for item in (1, 2):
        for h in (0, 1):
            far(h, item, shifts[item])
            keep(block_at(0, shifts[item], 1), h)
            keep(block_at(0, shifts[item], -1), h)
    for n, (src, dst) in enumerate(pairs):
        for step, slot in RELAY:
            part = pl.ds(2 * quarter + slot * (quarter // 2), quarter // 2)
            copies["relay", n, slot].wait_recv()
            begin(("relayed", n, slot), 48 + 2 * n + slot, (0, step), relay.at[n, slot], dst.at[part, :])
    for item in (3,):
        for h in (0, 1):
            far(h, item, shifts[item])
            keep(block_at(0, shifts[item], 1), h)
            keep(block_at(0, shifts[item], -1), h)
    for item in (0, 1, 2, 3):
        for h in (0, 1):
            copies[h, item, 2].wait_recv()
            copies[h, item, 3].wait_recv()
            keep(block_at(0, shifts[item], 2), h)
    for n in (0, 1):
        for name in (("move", n, 1), ("move", n, 3), ("relayed", n, 0), ("relayed", n, 1)):
            copies[name].wait_recv()
    for j in (1, 2, 3):
        copies["rows", j].wait_recv()
    for copy in stay + stores:
        copy.wait()
    for copy in copies.values():
        copy.wait_send()


def collect(keys, values, queries, out_grad, outputs):
    rows = keys.shape[0]
    heads = out_grad.shape[1] // HD
    bf = jnp.bfloat16
    vmem = pl.BlockSpec(memory_space=pltpu.VMEM)
    anywhere = pl.BlockSpec(memory_space=pl.ANY)
    return pl.pallas_call(
        collect_kernel,
        out_shape=[jax.ShapeDtypeStruct((SIDE * SIDE, rows, 2 * HD), bf),
                   jax.ShapeDtypeStruct(queries.shape, bf),
                   jax.ShapeDtypeStruct(queries.shape, bf),
                   jax.ShapeDtypeStruct((2 * heads, rows), jnp.float32)],
        in_specs=[anywhere] * 5,
        out_specs=[anywhere] * 3 + [vmem],
        scratch_shapes=[pltpu.VMEM((SIDE * SIDE, rows, 2 * HD), bf), pltpu.VMEM(keys.shape, bf), pltpu.VMEM(keys.shape, bf), pltpu.VMEM(queries.shape, bf), pltpu.VMEM(queries.shape, bf), pltpu.VMEM(queries.shape, bf),
                        pltpu.VMEM((2 * heads, rows), jnp.float32),
                        pltpu.VMEM((2, 2, rows // SIDE // 2, queries.shape[1]), bf),
                        pltpu.SemaphoreType.DMA((5,)), pltpu.SemaphoreType.DMA((2 * SIDE * SIDE,)), pltpu.SemaphoreType.DMA((55,)), pltpu.SemaphoreType.DMA((55,))],
        compiler_params=pltpu.CompilerParams(collective_id=0, has_side_effects=True, vmem_limit_bytes=62 * 2**20),
        name="collect",
    )(keys, values, queries, out_grad, outputs)


PARTS = 4
PART_ORDER = (0, 1, 3, 2)
FIRST_AXIS = ((0, 0), (0, 0), (0, 1), (0, 1))
RS_ORDER = (2, -1, 1, 0)


def tp_place(step, core):
    y = lax.axis_index("tp") // 2
    return lax.rem(y + step + SIDE, SIDE) * 2 + core


def finish_kernel(dq_in, dkv_hbm, wq_hbm, wk_hbm, wv_hbm, out_ref, dkv_ref, dq_ref, relay, wq_ref, wk_ref, wv_ref, wkv_ref, acc_ref, sum_ref,
                  low_ref, high_ref, stage_ref, fin_ref, res_ref, pair_out, pair_in, y_stage, y_low, y_high, y_fin,
                  load_sem, send_sem, recv_sem):
    core = lax.axis_index("tp") % 2
    rows = dq_ref.shape[0]
    part_rows = rows // PARTS
    size = part_rows // 2
    mid = size // 2
    loads = [
        pltpu.make_async_copy(dkv_hbm, dkv_ref, load_sem.at[0]),
        pltpu.make_async_copy(wq_hbm, wq_ref, load_sem.at[1]),
        pltpu.make_async_copy(wk_hbm, wk_ref, load_sem.at[2]),
        pltpu.make_async_copy(wv_hbm, wv_ref, load_sem.at[3]),
        pltpu.make_async_copy(dq_in.at[pl.ds(0, part_rows), :], dq_ref.at[pl.ds(0, part_rows), :], load_sem.at[4]),
    ]
    for copy in loads:
        copy.start()
    greet([{"ctx": ring_place(axis, step)} for axis in (0, 1) for step in (1, -1)]
          + [{"tp": tp_place(step, core)} for step in (1, -1)] + [{"tp": tp_place(0, 1 - core)}])
    copies = {}

    def begin(name, number, device, src, dst):
        copy = pltpu.make_async_remote_copy(src_ref=src, dst_ref=dst, send_sem=send_sem.at[number],
                                            recv_sem=recv_sem.at[number], device_id=device, device_id_type=MESH)
        copy.start()
        copies[name] = copy

    def wide(value):
        return value.astype(jnp.float32)

    def rows_of(s, h):
        return pl.ds(s * part_rows + h * size, size)

    def ident(s, h, k):
        return (s * 2 + h) * 5 + (4 if k is None else RS_ORDER.index(k))

    def term(s, h, k, shift, start, count, source=dkv_ref):
        if k is None:
            return res_ref.at[s, h, RS_ORDER.index(shift), pl.ds(start, count), :]
        return source.at[block_at(FIRST_AXIS[s][h], k, shift), pl.ds(s * part_rows + h * size + start, count), :]

    def ring_axis(s, h, k):
        return FIRST_AXIS[s][h] if k is None else 1 - FIRST_AXIS[s][h]

    def reduce_send(s, h, k):
        n, axis = ident(s, h, k), ring_axis(s, h, k)
        begin(("low", n), 4 * n, {"ctx": ring_place(axis, 1)}, term(s, h, k, 2, 0, mid, dkv_hbm),
              low_ref.at[n])
        begin(("high", n), 4 * n + 1, {"ctx": ring_place(axis, -1)}, term(s, h, k, 2, mid, mid, dkv_hbm),
              high_ref.at[n])

    def reduce_pass(s, h, k):
        n, axis = ident(s, h, k), ring_axis(s, h, k)
        copies["low", n].wait_recv()
        stage_ref[n, 0, :mid, :] = (wide(term(s, h, k, 1, 0, mid)[...]) + wide(low_ref[n])).astype(jnp.bfloat16)
        stage_ref[n, 0, mid:, :] = term(s, h, k, 1, mid, mid)[...]
        begin(("up", n), 4 * n + 2, {"ctx": ring_place(axis, 1)}, stage_ref.at[n, 0], fin_ref.at[n, 0])
        copies["high", n].wait_recv()
        stage_ref[n, 1, :mid, :] = term(s, h, k, -1, 0, mid)[...]
        stage_ref[n, 1, mid:, :] = (wide(term(s, h, k, -1, mid, mid)[...]) + wide(high_ref[n])).astype(jnp.bfloat16)
        begin(("down", n), 4 * n + 3, {"ctx": ring_place(axis, -1)}, stage_ref.at[n, 1], fin_ref.at[n, 1])

    def reduce_end(s, h, k):
        n = ident(s, h, k)
        copies["up", n].wait_recv()
        copies["down", n].wait_recv()
        total = wide(term(s, h, k, 0, 0, size)[...]) + wide(fin_ref[n, 0]) + wide(fin_ref[n, 1])
        if k is None:
            sum_ref[rows_of(s, h), :] = total.astype(jnp.bfloat16)
        else:
            res_ref[s, h, RS_ORDER.index(k)] = total.astype(jnp.bfloat16)

    def reduce_steps(s):
        for k in RS_ORDER:
            for h in (0, 1):
                reduce_send(s, h, k)
        yield
        for k in RS_ORDER:
            for h in (0, 1):
                reduce_pass(s, h, k)
        yield
        for h in (0, 1):
            reduce_end(s, h, 2)
            reduce_send(s, h, None)
        yield
        for h in (0, 1):
            reduce_end(s, h, -1)
            reduce_end(s, h, 1)
        for h in (0, 1):
            reduce_pass(s, h, None)
        yield
        for h in (0, 1):
            reduce_end(s, h, 0)
        yield
        for h in (0, 1):
            reduce_end(s, h, None)
        yield

    def project(g, n):
        part = pl.ds(n * (rows // 2), rows // 2)
        acc_ref[g, part, :] = lax.dot_general(dq_ref[part, :], wq_ref[g], LAST, preferred_element_type=jnp.float32)

    back = 48 * PARTS

    def give_back():
        for j, step in ((1, -1), (3, 1)):
            part = pl.ds(j * part_rows, part_rows)
            begin(("back", j), back + 2 + j // 2, {"ctx": ring_place(0, step)}, dq_in.at[part, :], dq_ref.at[part, :])
        for step, slot in RELAY:
            part = pl.ds(2 * part_rows + slot * size, size)
            begin(("relay", slot), back + slot, {"ctx": ring_place(0, step)}, dq_in.at[part, :], relay.at[slot])

    def relay_back():
        for step, slot in RELAY:
            part = pl.ds(2 * part_rows + slot * size, size)
            copies["relay", slot].wait_recv()
            begin(("relayed", slot), back + 4 + slot, {"ctx": ring_place(0, step)}, relay.at[slot], dq_ref.at[part, :])

    far = 40 * PARTS

    def spread(s, step):
        n = s * 4 + RS_ORDER.index(step)
        other, mine = tp_place(step, 1 - core), tp_place(step, core)
        part = pl.ds(s * part_rows, part_rows)
        low = sum_ref[part, :]
        total = acc_ref[other, part, :] + lax.dot_general(low, wkv_ref[other], LAST, preferred_element_type=jnp.float32)
        pair_out[n, 0] = total[:size].astype(jnp.bfloat16)
        pair_out[n, 1] = total[size:].astype(jnp.bfloat16)
        begin(("pair", n), far + n, {"tp": tp_place(0, 1 - core)}, pair_out.at[n], pair_in.at[n])
        acc_ref[mine, part, :] += lax.dot_general(low, wkv_ref[mine], LAST, preferred_element_type=jnp.float32)

    def chip_sum(s, step, h):
        n = s * 4 + RS_ORDER.index(step)
        return acc_ref[tp_place(step, core), rows_of(s, h), :] + wide(pair_in[n, h])

    def y_send(s):
        copies["pair", s * 4].wait_recv()
        for h in (0, 1):
            y_stage[s, 0, h] = chip_sum(s, 2, h).astype(jnp.bfloat16)
        number = far + 4 * PARTS + 4 * s
        begin(("y_low", s), number, {"tp": tp_place(1, core)}, y_stage.at[s, 0, 0], y_low.at[s])
        begin(("y_high", s), number + 1, {"tp": tp_place(-1, core)}, y_stage.at[s, 0, 1], y_high.at[s])

    def y_pass(s, step):
        number = far + 4 * PARTS + 4 * s
        copies["pair", s * 4 + RS_ORDER.index(step)].wait_recv()
        slot, low = (1, 0) if step == 1 else (2, 1)
        y_stage[s, slot, 1 - low] = chip_sum(s, step, 1 - low).astype(jnp.bfloat16)
        copies["y_low" if step == 1 else "y_high", s].wait_recv()
        came = y_low if step == 1 else y_high
        y_stage[s, slot, low] = (chip_sum(s, step, low) + wide(came[s])).astype(jnp.bfloat16)
        begin(("y_fin", s, step), number + 1 + slot, {"tp": tp_place(step, core)}, y_stage.at[s, slot],
              y_fin.at[s, slot - 1])

    def y_end(s):
        copies["pair", s * 4 + 3].wait_recv()
        copies["y_fin", s, 1].wait_recv()
        copies["y_fin", s, -1].wait_recv()
        for h in (0, 1):
            out_ref[rows_of(s, h), :] = (
                chip_sum(s, 0, h) + wide(y_fin[s, 0, h]) + wide(y_fin[s, 1, h])).astype(jnp.bfloat16)

    sums = {s: reduce_steps(s) for s in PART_ORDER}
    one, two, three, four = PART_ORDER
    next(sums[one])
    next(sums[two])
    give_back()
    next(sums[three])
    loads[0].wait()
    next(sums[one])
    next(sums[four])
    next(sums[two])
    loads[1].wait()
    loads[4].wait()
    copies["back", 1].wait_recv()
    for g in range(0, 2):
        project(g, 0)
    next(sums[one])
    next(sums[three])
    for g in range(2, 4):
        project(g, 0)
    next(sums[one])
    relay_back()
    next(sums[two])
    next(sums[four])
    for g in range(4, 6):
        project(g, 0)
    next(sums[one])
    for g in range(6, 8):
        project(g, 0)
    loads[2].wait()
    loads[3].wait()

    def merge(g, _):
        wkv_ref[g, :, :HD] = wk_ref[g]
        wkv_ref[g, :, HD:] = wv_ref[g]
        return 0

    lax.fori_loop(0, wkv_ref.shape[0], merge, 0)
    next(sums[one])
    next(sums[two])
    for step in RS_ORDER:
        spread(one, step)
    y_send(one)
    next(sums[two])
    next(sums[three])
    next(sums[two])
    next(sums[four])
    copies["back", 3].wait_recv()
    copies["relayed", 0].wait_recv()
    copies["relayed", 1].wait_recv()
    for g in range(0, 2):
        project(g, 1)
    next(sums[three])
    y_pass(one, 1)
    y_pass(one, -1)
    for g in range(2, 4):
        project(g, 1)
    for step in RS_ORDER:
        spread(two, step)
    y_send(two)
    next(sums[three])
    next(sums[four])
    for g in range(4, 6):
        project(g, 1)
    next(sums[three])
    next(sums[four])
    for g in range(6, 8):
        project(g, 1)
    y_pass(two, 1)
    y_pass(two, -1)
    for step in RS_ORDER:
        spread(three, step)
    y_send(three)
    next(sums[four])
    for step in RS_ORDER:
        spread(four, step)
    y_send(four)
    y_end(one)
    y_pass(three, 1)
    y_pass(three, -1)
    y_end(two)
    y_pass(four, 1)
    y_pass(four, -1)
    y_end(three)
    y_end(four)
    for copy in copies.values():
        copy.wait_send()


def finish(query_grad, terms, w_query, w_key, w_value):
    rows = query_grad.shape[0]
    blocks = SIDE * 2
    columns = w_query.shape[0] // blocks
    size = rows // PARTS // 2
    mid = size // 2
    reduces = 10 * PARTS
    sems = 4 * reduces + 8 * PARTS + 6
    bf = jnp.bfloat16
    vmem = pl.BlockSpec(memory_space=pltpu.VMEM)
    anywhere = pl.BlockSpec(memory_space=pl.ANY)
    return pl.pallas_call(
        finish_kernel,
        out_shape=jax.ShapeDtypeStruct((rows, columns), bf),
        in_specs=[anywhere] * 5,
        out_specs=vmem,
        scratch_shapes=[
            pltpu.VMEM(terms.shape, bf),
            pltpu.VMEM(query_grad.shape, bf),
            pltpu.VMEM((2, size, query_grad.shape[1]), bf),
            pltpu.VMEM((blocks, columns, w_query.shape[1]), bf),
            pltpu.VMEM((blocks, columns, HD), bf),
            pltpu.VMEM((blocks, columns, HD), bf),
            pltpu.VMEM((blocks, columns, 2 * HD), bf),
            pltpu.VMEM((blocks, rows, columns), jnp.float32),
            pltpu.VMEM((rows, 2 * HD), bf),
            pltpu.VMEM((reduces, mid, 2 * HD), bf),
            pltpu.VMEM((reduces, mid, 2 * HD), bf),
            pltpu.VMEM((reduces, 2, size, 2 * HD), bf),
            pltpu.VMEM((reduces, 2, size, 2 * HD), bf),
            pltpu.VMEM((PARTS, 2, 4, size, 2 * HD), bf),
            pltpu.VMEM((4 * PARTS, 2, size, columns), bf),
            pltpu.VMEM((4 * PARTS, 2, size, columns), bf),
            pltpu.VMEM((PARTS, 3, 2, size, columns), bf),
            pltpu.VMEM((PARTS, size, columns), bf),
            pltpu.VMEM((PARTS, size, columns), bf),
            pltpu.VMEM((PARTS, 2, 2, size, columns), bf),
            pltpu.SemaphoreType.DMA((5,)),
            pltpu.SemaphoreType.DMA((sems,)),
            pltpu.SemaphoreType.DMA((sems,)),
        ],
        compiler_params=pltpu.CompilerParams(collective_id=1, has_side_effects=True, vmem_limit_bytes=62 * 2**20),
        name="finish",
    )(query_grad, terms, w_query.reshape(blocks, columns, -1), w_key.reshape(blocks, columns, -1),
      w_value.reshape(blocks, columns, -1))


def work_start(j, rows):
    me = lax.axis_index("ctx")
    x, z = me // SIDE, me % SIDE
    return (lax.rem(x - j + SIDE, SIDE) * SIDE + z) * rows + j * CHUNK

def shards(queries, keys, values, outputs, out_grad, lengths, w_query, w_key, w_value):
    collected, q_work, grad_work, row_info = collect(keys, values, queries, out_grad, outputs)
    query_grad, terms = attention(lengths, q_work, grad_work, row_info, collected.reshape(-1, 2 * HD))
    return finish(query_grad, terms.reshape(collected.shape), w_query, w_key, w_value)


def solution(mesh):
    in_specs = (P("ctx", "tp"),) * 5 + (P(),) + (P(None, "tp"),) * 3
    return jax.shard_map(shards, mesh=mesh, in_specs=in_specs, out_specs=P("ctx", "tp"), check_vma=False)
```
